128 devices in a mesh: dp: 4 (over z_hi, core), ctx: 32 (over y, z_lo, x).
Axes of the slice: x: 4, y: 4, z: 4 (z_hi: 2, z_lo: 2; z = z_hi * 2 + z_lo), core: 2. Of those that a mesh axis runs over, the one named last changes fastest.
Arguments:
- query_rows: bfloat16 [16384, 8192], P(('dp', 'ctx')), parts along dimension 0, may hold values from -6 to 6
- key_rows: bfloat16 [16384, 8192], P(('dp', 'ctx')), parts along dimension 0, may hold values from -6 to 6
- value_rows: bfloat16 [16384, 8192], P(('dp', 'ctx')), parts along dimension 0, may hold values from -6 to 6
- short_taps: float32 [3, 3, 8192], replicated, may hold values from -3.5 to 3.5
- long_filter: float32 [4096, 8192], P(None, 'ctx'), may hold values from -0.09375 to 0.09375
- skip_gain: float32 [8192], P('ctx'), may hold values from 0.5 to 1.5
Outputs:
- mixed: bfloat16 [16384, 8192], P(('dp', 'ctx')), parts along dimension 0
The draws below stay inside these ranges and needn't reach their ends.
There are 4 independent parts, one for each index of `dp`. The reference program is written for one: setup_inputs(seed, part) draws one part's arguments, and reference() takes and returns one part's arrays. A program takes and returns all parts, laid end to end along the dimension named above; an argument that names none is the same for every part. Nothing has to cross between parts.
All inputs are finite; a program needn't handle non-finite values.
Results may differ from the reference program's by a relative error of at most 0.0058.
Values may be sent and summed in bfloat16 or wider, within the bound.
A program may use at most 192 MiB of HBM per device.

```python
import jax
import jax.numpy as jnp
from jax import lax

D = 8192
TAPS = 3
L = 4096


def levels(key, dims, cuts, smallest, largest):
    level = 1.0
    for axis_at, blocks in cuts:
        steps = jax.random.uniform(jax.random.fold_in(jax.random.fold_in(key, 6), axis_at), (blocks,), jnp.float32, smallest / len(cuts), largest / len(cuts))
        level = level * jnp.repeat(jnp.exp(steps), dims[axis_at] // blocks).reshape((-1,) + (1,) * (len(dims) - 1 - axis_at))
    return level


def gaussian(own_key, dims, scale, most, split=(), dtype=jnp.bfloat16):
    gain = levels(own_key, dims, split, -0.22, 0.18) if split else 1.0
    entries = jax.random.normal(own_key, dims, jnp.float32) * scale * gain
    return jnp.minimum(jnp.maximum(entries, -most), most).astype(dtype)


def setup_inputs(seed: int = 0, part: int = 0) -> dict:
    streams_of = jax.random.split(jax.random.key(seed), 7)
    own_keys = jax.random.split(jax.random.fold_in(streams_of[6], part), 7)
    return {
        "query_rows": gaussian(own_keys[0], (L, D), 1.0, 6.0, ((0, 32),)),
        "key_rows": gaussian(own_keys[1], (L, D), 1.0, 6.0, ((0, 32),)),
        "value_rows": gaussian(own_keys[2], (L, D), 1.0, 6.0, ((0, 32),)),
        "short_taps": gaussian(streams_of[3], (3, TAPS, D), TAPS ** -0.5, 3.5, (), jnp.float32),
        "long_filter": gaussian(streams_of[4], (L, D), L ** -0.5, 0.09375, ((1, 32),), jnp.float32),
        "skip_gain": jnp.clip(0.5 + 1.0 * jax.random.uniform(streams_of[5], (D,), jnp.float32) ** levels(streams_of[5], (D,), ((0, 32),), -0.2, 0.2), 0.5, 1.5),
    }


def causal_taps(signal, tap_weights):
    length = signal.shape[0]
    widened = jnp.concatenate([jnp.zeros((TAPS - 1, signal.shape[1]), jnp.float32), signal.astype(jnp.float32)], axis=0)
    result = jnp.zeros(signal.shape, jnp.float32)
    for offset in range(TAPS):
        result = result + tap_weights[offset] * widened[TAPS - 1 - offset:TAPS - 1 - offset + length]
    return result


def reference(query_rows, key_rows, value_rows, short_taps, long_filter, skip_gain):
    featured_q = causal_taps(query_rows, short_taps[0])
    featured_k = causal_taps(key_rows, short_taps[1])
    featured_v = causal_taps(value_rows, short_taps[2])
    gated = (featured_k * featured_v).astype(jnp.bfloat16)
    gated_wide = lax.optimization_barrier(gated).astype(jnp.float32)
    length = gated.shape[0]
    pieces = []
    for first_chan in range(0, D, 1024):
        last_chan = min(first_chan + 1024, D)
        spectrum = jnp.fft.rfft(gated_wide[:, first_chan:last_chan], n=2 * length, axis=0) * jnp.fft.rfft(long_filter[:, first_chan:last_chan], n=2 * length, axis=0)
        pieces.append(jnp.fft.irfft(spectrum, n=2 * length, axis=0)[:length])
    convolved = jnp.concatenate(pieces, axis=1) + skip_gain * gated_wide
    conv_out = lax.optimization_barrier(convolved.astype(jnp.bfloat16)).astype(jnp.float32)
    return (featured_q * conv_out).astype(jnp.bfloat16)
```

```python
import functools

import jax
import jax.numpy as jnp
import ml_dtypes
import numpy as np
from jax import lax
from jax.experimental import pallas as pl
from jax.experimental.pallas import tpu as pltpu
from jax.sharding import PartitionSpec as P

F32, BF16 = jnp.float32, jnp.bfloat16
MESH = pl.DeviceIdType.MESH

BLOCKS, ROWS, LANES = 32, 128, 128
FULL = 2 * BLOCKS * ROWS
HALVES = 2


def transform_tables():
    p, k1 = np.arange(BLOCKS), np.arange(BLOCKS)
    angle = 2 * np.pi * (k1[:, None] * p % 64) / 64
    outer = np.zeros((BLOCKS, 2, BLOCKS))
    outer[:, 0], outer[:, 1] = np.cos(angle), -np.sin(angle)
    outer[0, 1] = np.cos(np.pi * p)
    outer_back = np.zeros((BLOCKS, BLOCKS, 2))
    outer_back[:, :, 0], outer_back[:, :, 1] = 2 * np.cos(angle.T), -2 * np.sin(angle.T)
    outer_back[:, 0, 0], outer_back[:, 0, 1] = 1, np.cos(np.pi * p)
    outer_back /= FULL
    r, k2 = np.arange(ROWS), np.arange(ROWS)
    inner = np.zeros((BLOCKS, 2 * ROWS, 2 * ROWS))
    for k in range(1, BLOCKS):
        turn = 2 * np.pi * ((k + 64 * k2)[:, None] * r % FULL) / FULL
        cos, sin = np.cos(turn), np.sin(turn)
        inner[k] = np.block([[cos, sin], [-sin, cos]])
    half = np.arange(64)[:, None]
    even = 2 * np.pi * (64 * half * r % FULL) / FULL
    odd = 2 * np.pi * ((32 + 64 * half) * r % FULL) / FULL
    inner[0, 0:64, :ROWS], inner[0, 64:128, ROWS:] = np.cos(even), np.cos(odd)
    inner[0, 128:192, :ROWS], inner[0, 192:256, ROWS:] = -np.sin(even), -np.sin(odd)
    inner[0, 128, :ROWS] = np.cos(np.pi * r)
    inner_back = inner.transpose(0, 2, 1).copy()
    weight = np.full(2 * ROWS, 2.0)
    weight[0] = weight[128] = 1
    inner_back[0] *= weight
    eye = np.eye(8)
    outer = np.kron(outer.reshape(2 * BLOCKS, BLOCKS), eye)
    outer_back = np.kron(outer_back.reshape(BLOCKS, 2 * BLOCKS), eye)
    return outer, inner, inner_back, outer_back


def high_low(table):
    table = table.astype(np.float32)
    high = table.astype(ml_dtypes.bfloat16)
    return np.stack([high, (table - high.astype(np.float32)).astype(ml_dtypes.bfloat16)])


def high(table):
    return table.astype(np.float32).astype(ml_dtypes.bfloat16)


def dot(a, b):
    return jnp.dot(a, b, preferred_element_type=F32)


def split(a):
    top = a.astype(BF16)
    return top, (a - top.astype(F32)).astype(BF16)


def side_by_side(x, n):
    return jnp.concatenate([x[:, :8].reshape(8 * n, LANES), x[:, 8:].reshape(8 * n, LANES)], axis=1)


def stacked(z, n):
    return jnp.concatenate([z[:, :LANES].reshape(n, 8, LANES), z[:, LANES:].reshape(n, 8, LANES)], axis=1)


def loop(count, step, body):
    def several(j, carry):
        for i in range(step):
            body(j * step + i)
        return carry

    lax.fori_loop(0, count // step, several, 0)


def featurize(block, taps, edge_two, edge_one):
    row = lax.broadcasted_iota(jnp.int32, (8, LANES), 0)
    one, two = pltpu.roll(block, 1, 0), pltpu.roll(block, 2, 0)
    top_one = jnp.where(row == 0, edge_one, one[:8])
    top_two = jnp.where(row == 0, edge_two, jnp.where(row == 1, edge_one, two[:8]))
    one = jnp.concatenate([top_one, one[8:]], axis=0)
    two = jnp.concatenate([top_two, two[8:]], axis=0)
    return taps[0] * block + taps[1] * one + taps[2] * two


def kernel(
    query, key, value, short_taps, filt, skip, outer, inner, inner_back, outer_back, out,
    qbuf, kbuf, vbuf, taps, fbuf, sbuf, t_outer, t_inner, t_inner_back, t_outer_back,
    kv_out, kv_in, q_out, q_in, edges, gated, moved, conv, back,
    spec, spec_low, fspec, mid, featured, result,
    load_sem, edge_send, edge_recv, send_one, recv_one, send_two, recv_two, store_sem,
):
    me = lax.axis_index("ctx")
    x, z, y = me % 4, (me // 4) % 2, me // 8

    def partner(j):
        j = 31 - j
        dx, dz, dy = (j % 4), (j // 4) % 2, j // 8
        return (((y + dy) % 4) * 2 + (z + dz) % 2) * 4 + (x + dx) % 4

    barrier = pltpu.get_barrier_semaphore()

    def greet(j, carry):
        pl.semaphore_signal(barrier, inc=1, device_id={"ctx": (me + j) % BLOCKS}, device_id_type=MESH)
        return carry

    lax.fori_loop(1, BLOCKS, greet, 0)

    loads = [
        pltpu.make_async_copy(src, dst, load_sem.at[i])
        for i, (src, dst) in enumerate(
            [
                (key, kbuf), (value, vbuf), (query, qbuf), (short_taps, taps), (filt, fbuf), (outer, t_outer),
                (inner, t_inner), (skip, sbuf), (inner_back, t_inner_back), (outer_back, t_outer_back),
            ]
        )
    ]
    for load in loads:
        load.start()
    for i in (0, 1, 2):
        loads[i].wait()

    def last_rows(buf):
        return buf[ROWS - 16 :, :].astype(F32)[14:16]

    last_k, last_v, last_q = last_rows(kbuf), last_rows(vbuf), last_rows(qbuf)
    kv_out[...] = jnp.concatenate(
        [part[:, 1024 * s : 1024 * s + 1024] for s in range(8) for part in (last_k, last_v)], axis=0
    ).astype(BF16)
    q_out[...] = jnp.concatenate([last_q[:, 1024 * s : 1024 * s + 1024] for s in range(8)], axis=0).astype(BF16)
    pl.semaphore_wait(barrier, BLOCKS - 1)
    following = {"ctx": (me + 1) % BLOCKS}
    edge_copies = [
        pltpu.make_async_remote_copy(
            src_ref=src, dst_ref=dst, send_sem=edge_send.at[i], recv_sem=edge_recv.at[i],
            device_id=following, device_id_type=MESH,
        )
        for i, (src, dst) in enumerate([(kv_out, kv_in), (q_out, q_in)])
    ]
    for copy in edge_copies:
        copy.start()
    loads[3].wait()
    inside = jnp.where(me == 0, 0.0, 1.0)
    edge_copies[0].wait_recv()
    arrived = kv_in[...].astype(F32) * inside
    for s in range(8):
        edges[0:4, 1024 * s : 1024 * s + 1024] = arrived[4 * s : 4 * s + 4]

    def tap_rows(which, lanes):
        return [taps[which, i : i + 1, lanes] for i in range(3)]

    def to_channels(h, j):
        to = partner(j)
        return pltpu.make_async_remote_copy(
            src_ref=gated.at[h, to], dst_ref=moved.at[h, me], send_sem=send_one.at[h, to], recv_sem=recv_one.at[h, me],
            device_id={"ctx": to}, device_id_type=MESH,
        )

    for h in range(HALVES):
        def gate(to):
            lanes = pl.ds(pl.multiple_of((HALVES * to + h) * LANES, LANES), LANES)
            fk = featurize(kbuf[:, lanes].astype(F32), tap_rows(1, lanes), edges[0:1, lanes], edges[1:2, lanes])
            fv = featurize(vbuf[:, lanes].astype(F32), tap_rows(2, lanes), edges[2:3, lanes], edges[3:4, lanes])
            return (fk * fv).astype(BF16)

        def gate_and_send(j, carry):
            to = partner(j)
            gated[h, to] = gate(to)
            to_channels(h, j).start()
            return carry

        lax.fori_loop(0, BLOCKS - 1, gate_and_send, 0)
        moved[h, me] = gate(me)

    for i in range(4, 10):
        loads[i].wait()
    for h in range(HALVES):
        lanes = pl.ds(h * LANES, LANES)

        def filter_outer(g):
            rows = pl.ds(pl.multiple_of(16 * g, 16), 16)
            top, low = split(side_by_side(fbuf[:, rows, lanes], BLOCKS))
            turned = dot(t_outer[0], top) + dot(t_outer[1], top) + dot(t_outer[0], low)
            top, low = split(stacked(turned, 2 * BLOCKS))
            spec[:, rows, :] = top
            spec_low[:, rows, :] = low

        loop(8, 2, filter_outer)

        def filter_inner(k):
            slot = pl.ds(pl.multiple_of(2 * k, 2), 2)
            top = spec[slot].reshape(2 * ROWS, LANES)
            low = spec_low[slot].reshape(2 * ROWS, LANES)
            fspec[h, k] = dot(t_inner[0, k], top) + dot(t_inner[1, k], top) + dot(t_inner[0, k], low)

        loop(BLOCKS, 4, filter_inner)

    def to_positions(h, j):
        to = partner(j)
        return pltpu.make_async_remote_copy(
            src_ref=conv.at[h, to], dst_ref=back.at[h, me], send_sem=send_two.at[h, to], recv_sem=recv_two.at[h, me],
            device_id={"ctx": to}, device_id_type=MESH,
        )

    def arrival(src, dst, send, recv, h, origin):
        return pltpu.make_async_remote_copy(
            src_ref=src.at[h, origin], dst_ref=dst.at[h, origin], send_sem=send.at[h, origin],
            recv_sem=recv.at[h, origin], device_id={"ctx": origin}, device_id_type=MESH,
        )

    for h in range(HALVES):
        def await_gated(j, carry):
            arrival(gated, moved, send_one, recv_one, h, (me + j) % BLOCKS).wait_recv()
            return carry

        lax.fori_loop(1, BLOCKS, await_gated, 0)

        def signal_outer(g):
            rows = pl.ds(pl.multiple_of(16 * g, 16), 16)
            pairs = side_by_side(moved[h, :, rows, :].astype(F32), BLOCKS).astype(BF16)
            spec[:, rows, :] = stacked(dot(t_outer[0], pairs), 2 * BLOCKS).astype(BF16)

        loop(8, 2, signal_outer)

        def signal_inner(k):
            slot = pl.ds(pl.multiple_of(2 * k, 2), 2)
            signal = dot(t_inner[0, k], spec[slot].reshape(2 * ROWS, LANES))
            real, imag = signal[:ROWS], signal[ROWS:]
            f_real, f_imag = fspec[h, k, :ROWS], fspec[h, k, ROWS:]
            lone = (lax.broadcasted_iota(jnp.int32, (ROWS, LANES), 0) == 0) & (k == 0)
            f_last = jnp.where(lone, f_imag, f_real)
            f_imag = jnp.where(lone, 0.0, f_imag)
            product = jnp.concatenate([real * f_real - imag * f_imag, real * f_imag + imag * f_last], axis=0)
            mid[slot] = dot(t_inner_back[k], product.astype(BF16)).astype(BF16).reshape(2, ROWS, LANES)

        loop(BLOCKS, 8, signal_inner)
        gain = sbuf[:, h * LANES : (h + 1) * LANES]

        def signal_back(g):
            rows = pl.ds(pl.multiple_of(16 * g, 16), 16)
            pairs = side_by_side(mid[:, rows, :].astype(F32), 2 * BLOCKS).astype(BF16)
            restored = stacked(dot(t_outer_back[...], pairs), BLOCKS)
            conv[h, :, rows, :] = (restored + gain * moved[h, :, rows, :].astype(F32)).astype(BF16)

        loop(8, 2, signal_back)

        def send_back(j, carry):
            to_positions(h, j).start()
            return carry

        lax.fori_loop(0, BLOCKS - 1, send_back, 0)
        back[h, me] = conv[h, me]

    edge_copies[1].wait_recv()
    arrived_q = q_in[...].astype(F32) * inside
    for s in range(8):
        edges[4:6, 1024 * s : 1024 * s + 1024] = arrived_q[2 * s : 2 * s + 2]

    def feature_q(b, carry):
        lanes = pl.ds(pl.multiple_of(b * LANES, LANES), LANES)
        featured[:, lanes] = featurize(
            qbuf[:, lanes].astype(F32), tap_rows(0, lanes), edges[4:5, lanes], edges[5:6, lanes]
        )
        return carry

    lax.fori_loop(0, HALVES * BLOCKS, feature_q, 0)
    for h in range(HALVES):
        def store(origin):
            lanes = pl.ds(pl.multiple_of((HALVES * origin + h) * LANES, LANES), LANES)
            return pltpu.make_async_copy(result.at[:, lanes], out.at[:, lanes], store_sem.at[h, origin])

        def mix(origin):
            lanes = pl.ds(pl.multiple_of((HALVES * origin + h) * LANES, LANES), LANES)
            result[:, lanes] = (featured[:, lanes] * back[h, origin].astype(F32)).astype(BF16)
            store(origin).start()

        mix(me)

        def await_and_mix(j, carry):
            j = 31 - j
            dx, dz, dy = (j % 4), (j // 4) % 2, j // 8
            origin = (((y + 4 - dy) % 4) * 2 + (z + dz) % 2) * 4 + (x + 4 - dx) % 4
            arrival(conv, back, send_two, recv_two, h, origin).wait_recv()
            mix(origin)
            return carry

        lax.fori_loop(0, BLOCKS - 1, await_and_mix, 0)

    for copy in edge_copies:
        copy.wait_send()
    for h in range(HALVES):
        def finish(j, carry):
            to_channels(h, j).wait_send()
            to_positions(h, j).wait_send()
            return carry

        lax.fori_loop(0, BLOCKS - 1, finish, 0)

        def stored(origin, carry):
            lanes = pl.ds(pl.multiple_of((HALVES * origin + h) * LANES, LANES), LANES)
            pltpu.make_async_copy(result.at[:, lanes], out.at[:, lanes], store_sem.at[h, origin]).wait()
            return carry

        lax.fori_loop(0, BLOCKS, stored, 0)


def on_device(query_rows, key_rows, value_rows, short_taps, long_filter, skip_gain):
    rows, width = query_rows.shape
    outer, inner, inner_back, outer_back = transform_tables()
    tables = [high_low(outer), high_low(inner), high(inner_back), high(outer_back)]
    any_spec = pl.BlockSpec(memory_space=pl.ANY)
    dma = pltpu.SemaphoreType.DMA
    blocks = (HALVES, BLOCKS, ROWS, LANES)
    return pl.pallas_call(
        kernel,
        out_shape=jax.ShapeDtypeStruct((rows, width), BF16),
        in_specs=[any_spec] * 10,
        out_specs=any_spec,
        scratch_shapes=[
            pltpu.VMEM((rows, width), BF16), pltpu.VMEM((rows, width), BF16), pltpu.VMEM((rows, width), BF16),
            pltpu.VMEM((3, 3, width), F32), pltpu.VMEM((BLOCKS, ROWS, HALVES * LANES), F32), pltpu.VMEM((1, HALVES * LANES), F32),
            *[pltpu.VMEM(t.shape, BF16) for t in tables],
            pltpu.VMEM((32, 1024), BF16), pltpu.VMEM((32, 1024), BF16), pltpu.VMEM((16, 1024), BF16), pltpu.VMEM((16, 1024), BF16),
            pltpu.VMEM((8, width), F32),
            *[pltpu.VMEM(blocks, BF16)] * 4,
            pltpu.VMEM((2 * BLOCKS, ROWS, LANES), BF16), pltpu.VMEM((2 * BLOCKS, ROWS, LANES), BF16),
            pltpu.VMEM((HALVES, BLOCKS, 2 * ROWS, LANES), F32), pltpu.VMEM((2 * BLOCKS, ROWS, LANES), BF16),
            pltpu.VMEM((rows, width), F32), pltpu.VMEM((rows, width), BF16),
            dma((10,)), dma((2,)), dma((2,)), *[dma((HALVES, BLOCKS))] * 5,
        ],
        compiler_params=pltpu.CompilerParams(collective_id=0, has_side_effects=True, vmem_limit_bytes=62 << 20),
        name="mixer",
    )(
        query_rows, key_rows, value_rows, short_taps, long_filter.reshape(BLOCKS, ROWS, HALVES * LANES),
        skip_gain.reshape(1, HALVES * LANES), *[jnp.asarray(t) for t in tables],
    )


def solution(mesh):
    in_specs = (P(("dp", "ctx"), None), P(("dp", "ctx"), None), P(("dp", "ctx"), None), P(), P(None, "ctx"), P("ctx"))
    return jax.shard_map(on_device, mesh=mesh, in_specs=in_specs, out_specs=P(("dp", "ctx"), None), check_vma=False)
```

```python
import functools

import jax
import jax.numpy as jnp
import ml_dtypes
import numpy as np
from jax import lax
from jax.experimental import pallas as pl
from jax.experimental.pallas import tpu as pltpu
from jax.sharding import PartitionSpec as P

F32, BF16 = jnp.float32, jnp.bfloat16
MESH = pl.DeviceIdType.MESH

BLOCKS, ROWS, LANES = 32, 128, 128
FULL = 2 * BLOCKS * ROWS
HALVES = 2


def transform_tables():
    p, k1 = np.arange(BLOCKS), np.arange(BLOCKS)
    angle = 2 * np.pi * (k1[:, None] * p % 64) / 64
    outer = np.zeros((BLOCKS, 2, BLOCKS))
    outer[:, 0], outer[:, 1] = np.cos(angle), -np.sin(angle)
    outer[0, 1] = np.cos(np.pi * p)
    outer_back = np.zeros((BLOCKS, BLOCKS, 2))
    outer_back[:, :, 0], outer_back[:, :, 1] = 2 * np.cos(angle.T), -2 * np.sin(angle.T)
    outer_back[:, 0, 0], outer_back[:, 0, 1] = 1, np.cos(np.pi * p)
    outer_back /= FULL
    r, k2 = np.arange(ROWS), np.arange(ROWS)
    inner = np.zeros((BLOCKS, 2 * ROWS, 2 * ROWS))
    for k in range(1, BLOCKS):
        turn = 2 * np.pi * ((k + 64 * k2)[:, None] * r % FULL) / FULL
        cos, sin = np.cos(turn), np.sin(turn)
        inner[k] = np.block([[cos, sin], [-sin, cos]])
    half = np.arange(64)[:, None]
    even = 2 * np.pi * (64 * half * r % FULL) / FULL
    odd = 2 * np.pi * ((32 + 64 * half) * r % FULL) / FULL
    inner[0, 0:64, :ROWS], inner[0, 64:128, ROWS:] = np.cos(even), np.cos(odd)
    inner[0, 128:192, :ROWS], inner[0, 192:256, ROWS:] = -np.sin(even), -np.sin(odd)
    inner[0, 128, :ROWS] = np.cos(np.pi * r)
    inner_back = inner.transpose(0, 2, 1).copy()
    weight = np.full(2 * ROWS, 2.0)
    weight[0] = weight[128] = 1
    inner_back[0] *= weight
    eye = np.eye(8)
    outer = np.kron(outer.reshape(2 * BLOCKS, BLOCKS), eye)
    outer_back = np.kron(outer_back.reshape(BLOCKS, 2 * BLOCKS), eye)
    return outer, inner, inner_back, outer_back


def high_low(table):
    table = table.astype(np.float32)
    high = table.astype(ml_dtypes.bfloat16)
    return np.stack([high, (table - high.astype(np.float32)).astype(ml_dtypes.bfloat16)])


def high(table):
    return table.astype(np.float32).astype(ml_dtypes.bfloat16)


def dot(a, b):
    return jnp.dot(a, b, preferred_element_type=F32)


def split(a):
    top = a.astype(BF16)
    return top, (a - top.astype(F32)).astype(BF16)


def side_by_side(x, n):
    return jnp.concatenate([x[:, :8].reshape(8 * n, LANES), x[:, 8:].reshape(8 * n, LANES)], axis=1)


def stacked(z, n):
    return jnp.concatenate([z[:, :LANES].reshape(n, 8, LANES), z[:, LANES:].reshape(n, 8, LANES)], axis=1)


def loop(count, step, body):
    def several(j, carry):
        for i in range(step):
            body(j * step + i)
        return carry

    lax.fori_loop(0, count // step, several, 0)


def featurize(block, taps, edge_two, edge_one):
    row = lax.broadcasted_iota(jnp.int32, (8, LANES), 0)
    one, two = pltpu.roll(block, 1, 0), pltpu.roll(block, 2, 0)
    top_one = jnp.where(row == 0, edge_one, one[:8])
    top_two = jnp.where(row == 0, edge_two, jnp.where(row == 1, edge_one, two[:8]))
    one = jnp.concatenate([top_one, one[8:]], axis=0)
    two = jnp.concatenate([top_two, two[8:]], axis=0)
    return taps[0] * block + taps[1] * one + taps[2] * two


def offsets():
    span = [(dx, dy, dz) for dy in range(4) for dz in range(2) for dx in range(4)]
    return sorted(span, key=lambda o: -(min(o[0], 4 - o[0]) + min(o[1], 4 - o[1]) + o[2]))[:-1]


def kernel(
    query, key, value, short_taps, filt, skip, outer, inner, inner_back, outer_back, out,
    qbuf, kbuf, vbuf, taps, fbuf, sbuf, t_outer, t_inner, t_inner_back, t_outer_back,
    kv_out, kv_in, q_out, q_in, edges, gated, moved, conv, back,
    spec, spec_low, fspec, mid, featured,
    load_sem, edge_send, edge_recv, send_one, recv_one, send_top, recv_top, send_two, recv_two,
):
    me = lax.axis_index("ctx")
    x, z, y = me % 4, (me // 4) % 2, me // 8
    sign = 1 - 2 * (lax.axis_index("dp") % 2)

    def at(offset, way=1):
        dx, dy, dz = offset
        return ((y + 4 + way * sign * dy) % 4 * 2 + (z + dz) % 2) * 4 + (x + 4 + way * sign * dx) % 4

    barrier = pltpu.get_barrier_semaphore()

    def greet(j, carry):
        pl.semaphore_signal(barrier, inc=1, device_id={"ctx": (me + j) % BLOCKS}, device_id_type=MESH)
        return carry

    lax.fori_loop(1, BLOCKS, greet, 0)

    loads = [
        pltpu.make_async_copy(src, dst, load_sem.at[i])
        for i, (src, dst) in enumerate(
            [
                (key, kbuf), (value, vbuf), (short_taps, taps), (query, qbuf), (filt, fbuf), (outer, t_outer),
                (inner, t_inner), (skip, sbuf), (inner_back, t_inner_back), (outer_back, t_outer_back),
            ]
        )
    ]
    for i in (0, 1, 2):
        loads[i].start()
    for i in (0, 1, 2):
        loads[i].wait()
    for i in range(3, 10):
        loads[i].start()

    def last_rows(buf):
        return buf[ROWS - 16 :, :].astype(F32)[14:16]

    following = {"ctx": (me + 1) % BLOCKS}
    edge_copies = [
        pltpu.make_async_remote_copy(
            src_ref=src, dst_ref=dst, send_sem=edge_send.at[i], recv_sem=edge_recv.at[i],
            device_id=following, device_id_type=MESH,
        )
        for i, (src, dst) in enumerate([(kv_out, kv_in), (q_out, q_in)])
    ]
    inside = jnp.where(me == 0, 0.0, 1.0)
    last_k, last_v = last_rows(kbuf), last_rows(vbuf)
    kv_out[...] = jnp.concatenate(
        [part[:, 1024 * s : 1024 * s + 1024] for s in range(8) for part in (last_k, last_v)], axis=0
    ).astype(BF16)

    def lanes_of(owner, h):
        return pl.ds(pl.multiple_of((HALVES * owner + h) * LANES, LANES), LANES)

    def tap_rows(which, lanes):
        return [taps[which, i : i + 1, lanes] for i in range(3)]

    def gate(rows, lanes):
        none = jnp.zeros((1, LANES), F32)
        before = [edges[i : i + 1, lanes] for i in range(4)] if rows == 16 else [none] * 4
        fk = featurize(kbuf[:rows, lanes].astype(F32), tap_rows(1, lanes), before[0], before[1])
        fv = featurize(vbuf[:rows, lanes].astype(F32), tap_rows(2, lanes), before[2], before[3])
        return (fk * fv).astype(BF16)

    def copy_to(src, dst, send, recv, to, slots, theirs):
        return pltpu.make_async_remote_copy(
            src_ref=src, dst_ref=dst, send_sem=send.at[slots], recv_sem=recv.at[theirs],
            device_id={"ctx": to}, device_id_type=MESH,
        )

    def to_channels(h, to, origin):
        rows = pl.ds(16, ROWS - 16)
        return copy_to(gated.at[h, to, rows], moved.at[h, origin, rows], send_one, recv_one, to, (h, to), (h, origin))

    def tops(to, origin):
        rows = pl.ds(0, 16)
        return copy_to(gated.at[:, to, rows], moved.at[:, origin, rows], send_top, recv_top, to, to, origin)

    def to_positions(h, to, origin):
        return copy_to(conv.at[h, to], back.at[h, origin], send_two, recv_two, to, (h, to), (h, origin))

    for h in range(HALVES):
        def gate_rest(to, carry):
            gated[h, to, 16:] = gate(ROWS, lanes_of(to, h))[16:]
            return carry

        lax.fori_loop(0, BLOCKS, gate_rest, 0)
        if h == 0:
            pl.semaphore_wait(barrier, BLOCKS - 1)
            edge_copies[0].start()
        for offset in offsets():
            to_channels(h, at(offset), me).start()
        if h == 0:
            edge_copies[0].wait_recv()
            arrived = kv_in[...].astype(F32) * inside
            for s in range(8):
                edges[0:4, 1024 * s : 1024 * s + 1024] = arrived[4 * s : 4 * s + 4]

            def gate_top(to, carry):
                for half in range(HALVES):
                    gated[half, to, 0:16] = gate(16, lanes_of(to, half))
                return carry

            lax.fori_loop(0, BLOCKS, gate_top, 0)
            for offset in offsets():
                tops(at(offset), me).start()
    for h in range(HALVES):
        moved[h, me] = gated[h, me]

    for i in range(4, 10):
        loads[i].wait()

    def filter_spectrum(h):
        lanes = pl.ds(h * LANES, LANES)

        def filter_outer(g):
            rows = pl.ds(pl.multiple_of(16 * g, 16), 16)
            top, low = split(side_by_side(fbuf[:, rows, lanes], BLOCKS))
            turned = dot(t_outer[0], top) + dot(t_outer[1], top) + dot(t_outer[0], low)
            top, low = split(stacked(turned, 2 * BLOCKS))
            spec[:, rows, :] = top
            spec_low[:, rows, :] = low

        loop(8, 2, filter_outer)

        def filter_inner(k):
            slot = pl.ds(pl.multiple_of(2 * k, 2), 2)
            top = spec[slot].reshape(2 * ROWS, LANES)
            low = spec_low[slot].reshape(2 * ROWS, LANES)
            fspec[k] = dot(t_inner[0, k], top) + dot(t_inner[1, k], top) + dot(t_inner[0, k], low)

        loop(BLOCKS, 4, filter_inner)

    def convolve(h):
        def signal_outer(g):
            rows = pl.ds(pl.multiple_of(16 * g, 16), 16)
            pairs = side_by_side(moved[h, :, rows, :].astype(F32), BLOCKS).astype(BF16)
            spec[:, rows, :] = stacked(dot(t_outer[0], pairs), 2 * BLOCKS).astype(BF16)

        loop(8, 2, signal_outer)

        def signal_inner(k):
            slot = pl.ds(pl.multiple_of(2 * k, 2), 2)
            signal = dot(t_inner[0, k], spec[slot].reshape(2 * ROWS, LANES))
            real, imag = signal[:ROWS], signal[ROWS:]
            f_real, f_imag = fspec[k, :ROWS], fspec[k, ROWS:]
            lone = (lax.broadcasted_iota(jnp.int32, (ROWS, LANES), 0) == 0) & (k == 0)
            f_last = jnp.where(lone, f_imag, f_real)
            f_imag = jnp.where(lone, 0.0, f_imag)
            product = jnp.concatenate([real * f_real - imag * f_imag, real * f_imag + imag * f_last], axis=0)
            mid[slot] = dot(t_inner_back[k], product.astype(BF16)).astype(BF16).reshape(2, ROWS, LANES)

        loop(BLOCKS, 8, signal_inner)
        gain = sbuf[:, h * LANES : (h + 1) * LANES]

        def signal_back(g):
            rows = pl.ds(pl.multiple_of(16 * g, 16), 16)
            pairs = side_by_side(mid[:, rows, :].astype(F32), 2 * BLOCKS).astype(BF16)
            restored = stacked(dot(t_outer_back[...], pairs), BLOCKS)
            conv[h, :, rows, :] = (restored + gain * moved[h, :, rows, :].astype(F32)).astype(BF16)

        loop(8, 2, signal_back)

    def await_all(arrival):
        def one(j, carry):
            arrival((me + j) % BLOCKS).wait_recv()
            return carry

        lax.fori_loop(1, BLOCKS, one, 0)

    for h in range(HALVES):
        filter_spectrum(h)
        if h == 0:
            await_all(lambda origin: tops(origin, origin))
        await_all(lambda origin: to_channels(h, origin, origin))
        convolve(h)
        for offset in offsets():
            to_positions(h, at(offset), me).start()
        back[h, me] = conv[h, me]

    loads[3].wait()
    last_q = last_rows(qbuf)
    q_out[...] = jnp.concatenate([last_q[:, 1024 * s : 1024 * s + 1024] for s in range(8)], axis=0).astype(BF16)
    edge_copies[1].start()

    def feature_q(b, carry):
        lanes = pl.ds(pl.multiple_of(b * LANES, LANES), LANES)
        featured[:, lanes] = featurize(
            qbuf[:, lanes].astype(F32), tap_rows(0, lanes), edges[4:5, lanes], edges[5:6, lanes]
        )
        return carry

    edge_copies[1].wait_recv()
    arrived_q = q_in[...].astype(F32) * inside
    for s in range(8):
        edges[4:6, 1024 * s : 1024 * s + 1024] = arrived_q[2 * s : 2 * s + 2]
    lax.fori_loop(0, HALVES * BLOCKS, feature_q, 0)

    def mix(h, origin):
        lanes = lanes_of(origin, h)
        out[:, lanes] = (featured[:, lanes] * back[h, origin].astype(F32)).astype(BF16)

    for h in range(HALVES):
        mix(h, me)
        for offset in offsets():
            origin = at(offset, -1)
            to_positions(h, origin, origin).wait_recv()
            mix(h, origin)

    for copy in edge_copies:
        copy.wait_send()

    def finish(j, carry):
        to = (me + j) % BLOCKS
        tops(to, me).wait_send()
        for h in range(HALVES):
            to_channels(h, to, me).wait_send()
            to_positions(h, to, me).wait_send()
        return carry

    lax.fori_loop(1, BLOCKS, finish, 0)


def on_device(query_rows, key_rows, value_rows, short_taps, long_filter, skip_gain):
    rows, width = query_rows.shape
    outer, inner, inner_back, outer_back = transform_tables()
    tables = [high_low(outer), high_low(inner), high(inner_back), high(outer_back)]
    any_spec = pl.BlockSpec(memory_space=pl.ANY)
    dma = pltpu.SemaphoreType.DMA
    blocks = (HALVES, BLOCKS, ROWS, LANES)
    return pl.pallas_call(
        kernel,
        out_shape=pltpu.VMEM((rows, width), BF16),
        in_specs=[any_spec] * 10,
        out_specs=pl.BlockSpec(memory_space=pltpu.VMEM),
        scratch_shapes=[
            pltpu.VMEM((rows, width), BF16), pltpu.VMEM((rows, width), BF16), pltpu.VMEM((rows, width), BF16),
            pltpu.VMEM((3, 3, width), F32), pltpu.VMEM((BLOCKS, ROWS, HALVES * LANES), F32), pltpu.VMEM((1, HALVES * LANES), F32),
            *[pltpu.VMEM(t.shape, BF16) for t in tables],
            pltpu.VMEM((32, 1024), BF16), pltpu.VMEM((32, 1024), BF16), pltpu.VMEM((16, 1024), BF16), pltpu.VMEM((16, 1024), BF16),
            pltpu.VMEM((8, width), F32),
            *[pltpu.VMEM(blocks, BF16)] * 4,
            pltpu.VMEM((2 * BLOCKS, ROWS, LANES), BF16), pltpu.VMEM((2 * BLOCKS, ROWS, LANES), BF16),
            pltpu.VMEM((BLOCKS, 2 * ROWS, LANES), F32), pltpu.VMEM((2 * BLOCKS, ROWS, LANES), BF16),
            pltpu.VMEM((rows, width), F32),
            dma((10,)), dma((2,)), dma((2,)), *[dma((HALVES, BLOCKS))] * 2, *[dma((BLOCKS,))] * 2, *[dma((HALVES, BLOCKS))] * 2,
        ],
        compiler_params=pltpu.CompilerParams(collective_id=0, has_side_effects=True, vmem_limit_bytes=56 << 20),
        name="mixer",
    )(
        query_rows, key_rows, value_rows, short_taps, long_filter.reshape(BLOCKS, ROWS, HALVES * LANES),
        skip_gain.reshape(1, HALVES * LANES), *[jnp.asarray(t) for t in tables],
    )


def solution(mesh):
    in_specs = (P(("dp", "ctx"), None), P(("dp", "ctx"), None), P(("dp", "ctx"), None), P(), P(None, "ctx"), P("ctx"))
    return jax.shard_map(on_device, mesh=mesh, in_specs=in_specs, out_specs=P(("dp", "ctx"), None), check_vma=False)
```

```python
import functools

import jax
import jax.numpy as jnp
import ml_dtypes
import numpy as np
from jax import lax
from jax.experimental import pallas as pl
from jax.experimental.pallas import tpu as pltpu
from jax.sharding import PartitionSpec as P

F32, BF16 = jnp.float32, jnp.bfloat16
MESH = pl.DeviceIdType.MESH

BLOCKS, ROWS, LANES = 32, 128, 128
FULL = 2 * BLOCKS * ROWS
HALVES = 2


def transform_tables():
    p, k1 = np.arange(BLOCKS), np.arange(BLOCKS)
    angle = 2 * np.pi * (k1[:, None] * p % 64) / 64
    outer = np.zeros((BLOCKS, 2, BLOCKS))
    outer[:, 0], outer[:, 1] = np.cos(angle), -np.sin(angle)
    outer[0, 1] = np.cos(np.pi * p)
    outer_back = np.zeros((BLOCKS, BLOCKS, 2))
    outer_back[:, :, 0], outer_back[:, :, 1] = 2 * np.cos(angle.T), -2 * np.sin(angle.T)
    outer_back[:, 0, 0], outer_back[:, 0, 1] = 1, np.cos(np.pi * p)
    outer_back /= FULL
    r, k2 = np.arange(ROWS), np.arange(ROWS)
    inner = np.zeros((BLOCKS, 2 * ROWS, 2 * ROWS))
    for k in range(1, BLOCKS):
        turn = 2 * np.pi * ((k + 64 * k2)[:, None] * r % FULL) / FULL
        cos, sin = np.cos(turn), np.sin(turn)
        inner[k] = np.block([[cos, sin], [-sin, cos]])
    half = np.arange(64)[:, None]
    even = 2 * np.pi * (64 * half * r % FULL) / FULL
    odd = 2 * np.pi * ((32 + 64 * half) * r % FULL) / FULL
    inner[0, 0:64, :ROWS], inner[0, 64:128, ROWS:] = np.cos(even), np.cos(odd)
    inner[0, 128:192, :ROWS], inner[0, 192:256, ROWS:] = -np.sin(even), -np.sin(odd)
    inner[0, 128, :ROWS] = np.cos(np.pi * r)
    inner_back = inner.transpose(0, 2, 1).copy()
    weight = np.full(2 * ROWS, 2.0)
    weight[0] = weight[128] = 1
    inner_back[0] *= weight
    eye = np.eye(8)
    outer = np.kron(outer.reshape(2 * BLOCKS, BLOCKS), eye)
    outer_back = np.kron(outer_back.reshape(BLOCKS, 2 * BLOCKS), eye)
    return outer, inner, inner_back, outer_back


def high_low(table):
    table = table.astype(np.float32)
    high = table.astype(ml_dtypes.bfloat16)
    return np.stack([high, (table - high.astype(np.float32)).astype(ml_dtypes.bfloat16)])


def high(table):
    return table.astype(np.float32).astype(ml_dtypes.bfloat16)


def dot(a, b):
    return jnp.dot(a, b, preferred_element_type=F32)


def split(a):
    top = a.astype(BF16)
    return top, (a - top.astype(F32)).astype(BF16)


def side_by_side(x, n):
    return jnp.concatenate([x[:, :8].reshape(8 * n, LANES), x[:, 8:].reshape(8 * n, LANES)], axis=1)


def stacked(z, n):
    return jnp.concatenate([z[:, :LANES].reshape(n, 8, LANES), z[:, LANES:].reshape(n, 8, LANES)], axis=1)


def loop(count, step, body):
    def several(j, carry):
        for i in range(step):
            body(j * step + i)
        return carry

    lax.fori_loop(0, count // step, several, 0)


def featurize(block, taps, edge_two, edge_one):
    row = lax.broadcasted_iota(jnp.int32, (8, LANES), 0)
    one, two = pltpu.roll(block, 1, 0), pltpu.roll(block, 2, 0)
    top_one = jnp.where(row == 0, edge_one, one[:8])
    top_two = jnp.where(row == 0, edge_two, jnp.where(row == 1, edge_one, two[:8]))
    one = jnp.concatenate([top_one, one[8:]], axis=0)
    two = jnp.concatenate([top_two, two[8:]], axis=0)
    return taps[0] * block + taps[1] * one + taps[2] * two


def offsets():
    span = [(dx, dy, dz) for dy in range(4) for dz in range(2) for dx in range(4)]
    return sorted(span, key=lambda o: -(min(o[0], 4 - o[0]) + min(o[1], 4 - o[1]) + o[2]))[:-1]


def kernel(
    query, key, value, short_taps, filt, skip, outer, inner, inner_back, outer_back, out,
    qbuf, kbuf, vbuf, taps, fbuf, sbuf, t_outer, t_inner, t_inner_back, t_outer_back,
    edge_out, edge_in, edges, gated, moved, conv, back, spec, spec_low, fspec,
    load_sem, edge_send, edge_recv, send_one, recv_one, send_two, recv_two,
):
    me = lax.axis_index("ctx")
    x, z, y = me % 4, (me // 4) % 2, me // 8
    sign = 1 - 2 * (lax.axis_index("dp") % 2)

    def at(offset, way=1):
        dx, dy, dz = offset
        return ((y + 4 + way * sign * dy) % 4 * 2 + (z + dz) % 2) * 4 + (x + 4 + way * sign * dx) % 4

    barrier = pltpu.get_barrier_semaphore()

    def greet(j, carry):
        pl.semaphore_signal(barrier, inc=1, device_id={"ctx": (me + j) % BLOCKS}, device_id_type=MESH)
        return carry

    lax.fori_loop(1, BLOCKS, greet, 0)

    loads = [
        pltpu.make_async_copy(src, dst, load_sem.at[i])
        for i, (src, dst) in enumerate(
            [
                (key, kbuf), (value, vbuf), (short_taps, taps), (query, qbuf), (filt, fbuf), (outer, t_outer),
                (inner, t_inner), (skip, sbuf), (inner_back, t_inner_back), (outer_back, t_outer_back),
            ]
        )
    ]
    for i in (0, 1, 2):
        loads[i].start()
    for i in (0, 1, 2):
        loads[i].wait()
    for i in range(3, 10):
        loads[i].start()

    def last_rows(buf, h):
        rows = buf[ROWS - 16 :, :].astype(F32)[14:16]
        picked = [rows[:, (HALVES * b + h) * LANES : (HALVES * b + h + 1) * LANES] for b in range(BLOCKS)]
        return [jnp.concatenate(picked[8 * s : 8 * s + 8], axis=1) for s in range(4)]

    following = {"ctx": (me + 1) % BLOCKS}
    edge_copies = [
        pltpu.make_async_remote_copy(
            src_ref=edge_out.at[i], dst_ref=edge_in.at[i], send_sem=edge_send.at[i], recv_sem=edge_recv.at[i],
            device_id=following, device_id_type=MESH,
        )
        for i in range(3)
    ]
    inside = jnp.where(me == 0, 0.0, 1.0)
    for h in range(HALVES):
        parts = [part for both in zip(last_rows(kbuf, h), last_rows(vbuf, h)) for part in both]
        edge_out[h] = jnp.concatenate(parts, axis=0).astype(BF16)

    def lanes_of(owner, h):
        return pl.ds(pl.multiple_of((HALVES * owner + h) * LANES, LANES), LANES)

    def block_lanes(owner):
        return pl.ds(pl.multiple_of(owner * LANES, LANES), LANES)

    def tap_rows(which, lanes):
        return [taps[which, i : i + 1, lanes] for i in range(3)]

    def gate(rows, owner, h):
        lanes = lanes_of(owner, h)
        if rows == 16:
            before = [edges[h, i : i + 1, block_lanes(owner)] for i in range(4)]
        else:
            before = [jnp.zeros((1, LANES), F32)] * 4
        fk = featurize(kbuf[:rows, lanes].astype(F32), tap_rows(1, lanes), before[0], before[1])
        fv = featurize(vbuf[:rows, lanes].astype(F32), tap_rows(2, lanes), before[2], before[3])
        return (fk * fv).astype(BF16)

    def copy_to(src, dst, send, recv, to, h, origin):
        return pltpu.make_async_remote_copy(
            src_ref=src.at[h, to], dst_ref=dst.at[h, origin], send_sem=send.at[h, to], recv_sem=recv.at[h, origin],
            device_id={"ctx": to}, device_id_type=MESH,
        )

    def to_channels(h, to, origin):
        return copy_to(gated, moved, send_one, recv_one, to, h, origin)

    def to_positions(h, to, origin):
        return copy_to(conv, back, send_two, recv_two, to, h, origin)

    def gate_rest(h):
        def one(owner, carry):
            gated[h, owner, 16:] = gate(ROWS, owner, h)[16:]
            return carry

        lax.fori_loop(0, BLOCKS, one, 0)

    def gate_top(h):
        arrived = edge_in[h].astype(F32) * inside
        for s in range(4):
            edges[h, 0:4, 1024 * s : 1024 * s + 1024] = arrived[4 * s : 4 * s + 4]

        def one(owner, carry):
            gated[h, owner, :16] = gate(16, owner, h)
            return carry

        lax.fori_loop(0, BLOCKS, one, 0)

    gate_rest(0)
    pl.semaphore_wait(barrier, BLOCKS - 1)
    for h in range(HALVES):
        edge_copies[h].start()
    gate_rest(1)
    for h in range(HALVES):
        edge_copies[h].wait_recv()
        gate_top(h)
        for offset in offsets():
            to_channels(h, at(offset), me).start()
    for h in range(HALVES):
        moved[h, me] = gated[h, me]
    loads[3].wait()
    edge_out[2] = jnp.concatenate([part for h in range(HALVES) for part in last_rows(qbuf, h)], axis=0).astype(BF16)
    edge_copies[2].start()

    for i in range(4, 10):
        loads[i].wait()

    def filter_outer(g):
        turned = []
        for i in range(2):
            rows = pl.ds(pl.multiple_of(16 * g + 8 * i, 8), 8)
            top, low = split(fbuf[:, rows, :].reshape(8 * BLOCKS, HALVES * LANES))
            part = dot(t_outer[0], top) + dot(t_outer[1], top) + dot(t_outer[0], low)
            turned.append(part.reshape(2 * BLOCKS, 8, HALVES * LANES))
        top, low = split(jnp.concatenate(turned, axis=1))
        rows = pl.ds(pl.multiple_of(16 * g, 16), 16)
        spec[:, rows, :] = top
        spec_low[:, rows, :] = low

    loop(8, 2, filter_outer)

    def filter_inner(k):
        slot = pl.ds(pl.multiple_of(2 * k, 2), 2)
        top = spec[slot].reshape(2 * ROWS, HALVES * LANES)
        low = spec_low[slot].reshape(2 * ROWS, HALVES * LANES)
        fspec[k] = dot(t_inner[0, k], top) + dot(t_inner[1, k], top) + dot(t_inner[0, k], low)

    loop(BLOCKS, 8, filter_inner)

    edge_copies[2].wait_recv()
    arrived_q = edge_in[2].astype(F32) * inside
    for h in range(HALVES):
        for s in range(4):
            row = 8 * h + 2 * s
            edges[h, 4:6, 1024 * s : 1024 * s + 1024] = arrived_q[row : row + 2]

    def feature_q(owner, carry):
        for h in range(HALVES):
            lanes = lanes_of(owner, h)
            before = [edges[h, i : i + 1, block_lanes(owner)] for i in (4, 5)]
            fbuf[owner, :, h * LANES : (h + 1) * LANES] = featurize(
                qbuf[:, lanes].astype(F32), tap_rows(0, lanes), before[0], before[1]
            )
        return carry

    def convolve(h):
        half = pl.ds(h * LANES, LANES)
        first = pl.ds(0, LANES)

        def signal_outer(g):
            rows = pl.ds(pl.multiple_of(16 * g, 16), 16)
            pairs = side_by_side(moved[h, :, rows, :].astype(F32), BLOCKS).astype(BF16)
            spec[:, rows, first] = stacked(dot(t_outer[0], pairs), 2 * BLOCKS).astype(BF16)

        loop(8, 4, signal_outer)

        def signal_inner(k):
            slot = pl.ds(pl.multiple_of(2 * k, 2), 2)
            signal = dot(t_inner[0, k], spec[slot, :, first].reshape(2 * ROWS, LANES))
            real, imag = signal[:ROWS], signal[ROWS:]
            f_real, f_imag = fspec[k, :ROWS, half], fspec[k, ROWS:, half]
            lone = (lax.broadcasted_iota(jnp.int32, (ROWS, LANES), 0) == 0) & (k == 0)
            f_last = jnp.where(lone, f_imag, f_real)
            f_imag = jnp.where(lone, 0.0, f_imag)
            product = jnp.concatenate([real * f_real - imag * f_imag, real * f_imag + imag * f_last], axis=0)
            restored = dot(t_inner_back[k], product.astype(BF16)).astype(BF16)
            spec_low[slot, :, first] = restored.reshape(2, ROWS, LANES)

        loop(BLOCKS, 8, signal_inner)
        gain = sbuf[:, h * LANES : (h + 1) * LANES]

        def signal_back(g):
            rows = pl.ds(pl.multiple_of(16 * g, 16), 16)
            pairs = side_by_side(spec_low[:, rows, first].astype(F32), 2 * BLOCKS).astype(BF16)
            restored = stacked(dot(t_outer_back[...], pairs), BLOCKS)
            conv[h, :, rows, :] = (restored + gain * moved[h, :, rows, :].astype(F32)).astype(BF16)

        loop(8, 4, signal_back)

    for h in range(HALVES):
        def await_gated(j, carry):
            origin = (me + j) % BLOCKS
            to_channels(h, origin, origin).wait_recv()
            return carry

        lax.fori_loop(1, BLOCKS, await_gated, 0)
        convolve(h)
        for offset in offsets():
            to_positions(h, at(offset), me).start()
        back[h, me] = conv[h, me]

    lax.fori_loop(0, BLOCKS, feature_q, 0)

    def mix(h, origin):
        features = fbuf[origin, :, h * LANES : (h + 1) * LANES]
        out[:, lanes_of(origin, h)] = (features * back[h, origin].astype(F32)).astype(BF16)

    for h in range(HALVES):
        mix(h, me)
        for offset in offsets():
            origin = at(offset, -1)
            to_positions(h, origin, origin).wait_recv()
            mix(h, origin)

    for copy in edge_copies:
        copy.wait_send()

    def finish(j, carry):
        to = (me + j) % BLOCKS
        for h in range(HALVES):
            to_channels(h, to, me).wait_send()
            to_positions(h, to, me).wait_send()
        return carry

    lax.fori_loop(1, BLOCKS, finish, 0)


def on_device(query_rows, key_rows, value_rows, short_taps, long_filter, skip_gain):
    rows, width = query_rows.shape
    outer, inner, inner_back, outer_back = transform_tables()
    tables = [high_low(outer), high_low(inner), high(inner_back), high(outer_back)]
    any_spec = pl.BlockSpec(memory_space=pl.ANY)
    dma = pltpu.SemaphoreType.DMA
    blocks = (HALVES, BLOCKS, ROWS, LANES)
    return pl.pallas_call(
        kernel,
        out_shape=pltpu.VMEM((rows, width), BF16),
        in_specs=[any_spec] * 10,
        out_specs=pl.BlockSpec(memory_space=pltpu.VMEM),
        scratch_shapes=[
            pltpu.VMEM((rows, width), BF16), pltpu.VMEM((rows, width), BF16), pltpu.VMEM((rows, width), BF16),
            pltpu.VMEM((3, 3, width), F32), pltpu.VMEM((BLOCKS, ROWS, HALVES * LANES), F32), pltpu.VMEM((1, HALVES * LANES), F32),
            *[pltpu.VMEM(t.shape, BF16) for t in tables],
            pltpu.VMEM((3, 16, 1024), BF16), pltpu.VMEM((3, 16, 1024), BF16), pltpu.VMEM((HALVES, 8, width // HALVES), F32),
            *[pltpu.VMEM(blocks, BF16)] * 4,
            *[pltpu.VMEM((2 * BLOCKS, ROWS, HALVES * LANES), BF16)] * 2,
            pltpu.VMEM((BLOCKS, 2 * ROWS, HALVES * LANES), F32),
            dma((10,)), dma((3,)), dma((3,)), *[dma((HALVES, BLOCKS))] * 4,
        ],
        compiler_params=pltpu.CompilerParams(collective_id=0, has_side_effects=True, vmem_limit_bytes=56 << 20),
        name="mixer",
    )(
        query_rows, key_rows, value_rows, short_taps, long_filter.reshape(BLOCKS, ROWS, HALVES * LANES),
        skip_gain.reshape(1, HALVES * LANES), *[jnp.asarray(t) for t in tables],
    )


def solution(mesh):
    in_specs = (P(("dp", "ctx"), None), P(("dp", "ctx"), None), P(("dp", "ctx"), None), P(), P(None, "ctx"), P("ctx"))
    return jax.shard_map(on_device, mesh=mesh, in_specs=in_specs, out_specs=P(("dp", "ctx"), None), check_vma=False)
```

```python
import functools

import jax
import jax.numpy as jnp
import ml_dtypes
import numpy as np
from jax import lax
from jax.experimental import pallas as pl
from jax.experimental.pallas import tpu as pltpu
from jax.sharding import PartitionSpec as P

F32, BF16 = jnp.float32, jnp.bfloat16
MESH = pl.DeviceIdType.MESH

BLOCKS, ROWS, LANES = 32, 128, 128
FULL = 2 * BLOCKS * ROWS
HALVES = 2


def transform_tables():
    p, k1 = np.arange(BLOCKS), np.arange(BLOCKS)
    angle = 2 * np.pi * (k1[:, None] * p % 64) / 64
    outer = np.zeros((BLOCKS, 2, BLOCKS))
    outer[:, 0], outer[:, 1] = np.cos(angle), -np.sin(angle)
    outer[0, 1] = np.cos(np.pi * p)
    outer_back = np.zeros((BLOCKS, BLOCKS, 2))
    outer_back[:, :, 0], outer_back[:, :, 1] = 2 * np.cos(angle.T), -2 * np.sin(angle.T)
    outer_back[:, 0, 0], outer_back[:, 0, 1] = 1, np.cos(np.pi * p)
    outer_back /= FULL
    r, k2 = np.arange(ROWS), np.arange(ROWS)
    inner = np.zeros((BLOCKS, 2 * ROWS, 2 * ROWS))
    for k in range(1, BLOCKS):
        turn = 2 * np.pi * ((k + 64 * k2)[:, None] * r % FULL) / FULL
        cos, sin = np.cos(turn), np.sin(turn)
        inner[k] = np.block([[cos, sin], [-sin, cos]])
    half = np.arange(64)[:, None]
    even = 2 * np.pi * (64 * half * r % FULL) / FULL
    odd = 2 * np.pi * ((32 + 64 * half) * r % FULL) / FULL
    inner[0, 0:64, :ROWS], inner[0, 64:128, ROWS:] = np.cos(even), np.cos(odd)
    inner[0, 128:192, :ROWS], inner[0, 192:256, ROWS:] = -np.sin(even), -np.sin(odd)
    inner[0, 128, :ROWS] = np.cos(np.pi * r)
    inner_back = inner.transpose(0, 2, 1).copy()
    weight = np.full(2 * ROWS, 2.0)
    weight[0] = weight[128] = 1
    inner_back[0] *= weight
    eye = np.eye(8)
    outer = np.kron(outer.reshape(2 * BLOCKS, BLOCKS), eye)
    outer_back = np.kron(outer_back.reshape(BLOCKS, 2 * BLOCKS), eye)
    return outer, inner, inner_back, outer_back


def high_low(table):
    table = table.astype(np.float32)
    high = table.astype(ml_dtypes.bfloat16)
    return np.stack([high, (table - high.astype(np.float32)).astype(ml_dtypes.bfloat16)])


def high(table):
    return table.astype(np.float32).astype(ml_dtypes.bfloat16)


def dot(a, b):
    return jnp.dot(a, b, preferred_element_type=F32)


def split(a):
    top = a.astype(BF16)
    return top, (a - top.astype(F32)).astype(BF16)


def side_by_side(x, n):
    return jnp.concatenate([x[:, :8].reshape(8 * n, LANES), x[:, 8:].reshape(8 * n, LANES)], axis=1)


def stacked(z, n):
    return jnp.concatenate([z[:, :LANES].reshape(n, 8, LANES), z[:, LANES:].reshape(n, 8, LANES)], axis=1)


def loop(count, step, body):
    def several(j, carry):
        for i in range(step):
            body(j * step + i)
        return carry

    lax.fori_loop(0, count // step, several, 0)


def featurize(block, taps, edge_two, edge_one):
    row = lax.broadcasted_iota(jnp.int32, (8, LANES), 0)
    one, two = pltpu.roll(block, 1, 0), pltpu.roll(block, 2, 0)
    top_one = jnp.where(row == 0, edge_one, one[:8])
    top_two = jnp.where(row == 0, edge_two, jnp.where(row == 1, edge_one, two[:8]))
    one = jnp.concatenate([top_one, one[8:]], axis=0)
    two = jnp.concatenate([top_two, two[8:]], axis=0)
    return taps[0] * block + taps[1] * one + taps[2] * two


def offsets():
    span = [(dx, dy, dz) for dy in range(4) for dz in range(2) for dx in range(4)]
    far = sorted(span, key=lambda o: -(min(o[0], 4 - o[0]) + min(o[1], 4 - o[1]) + o[2]))[:-1]
    return [far[j // 2] if j % 2 == 0 else far[-1 - j // 2] for j in range(31)]


def kernel(
    query, key, value, short_taps, filt, skip, outer, inner, inner_back, outer_back, out,
    qbuf, kbuf, vbuf, taps, fbuf, sbuf, t_outer, t_inner, t_inner_back, t_outer_back,
    edge_out, edge_in, edges, gated, moved, conv, back, spec, spec_low, fspec,
    load_sem, edge_send, edge_recv, send_one, recv_one, send_two, recv_two,
):
    me = lax.axis_index("ctx")
    x, z, y = me % 4, (me // 4) % 2, me // 8
    sign = 1 - 2 * (lax.axis_index("dp") % 2)

    def at(offset, way=1):
        dx, dy, dz = offset
        return ((y + 4 + way * sign * dy) % 4 * 2 + (z + dz) % 2) * 4 + (x + 4 + way * sign * dx) % 4

    barrier = pltpu.get_barrier_semaphore()

    def greet(j, carry):
        pl.semaphore_signal(barrier, inc=1, device_id={"ctx": (me + j) % BLOCKS}, device_id_type=MESH)
        return carry

    lax.fori_loop(1, BLOCKS, greet, 0)

    loads = [
        pltpu.make_async_copy(src, dst, load_sem.at[i])
        for i, (src, dst) in enumerate(
            [
                (key, kbuf), (value, vbuf), (short_taps, taps), (query, qbuf), (filt, fbuf), (outer, t_outer),
                (inner, t_inner), (skip, sbuf), (inner_back, t_inner_back), (outer_back, t_outer_back),
            ]
        )
    ]
    for i in (0, 1, 2):
        loads[i].start()
    for i in (0, 1, 2):
        loads[i].wait()
    loads[4].start()

    def last_rows(buf, h):
        rows = buf[ROWS - 16 :, :].astype(F32)[14:16]
        picked = [rows[:, (HALVES * b + h) * LANES : (HALVES * b + h + 1) * LANES] for b in range(BLOCKS)]
        return [jnp.concatenate(picked[8 * s : 8 * s + 8], axis=1) for s in range(4)]

    following = {"ctx": (me + 1) % BLOCKS}
    edge_copies = [
        pltpu.make_async_remote_copy(
            src_ref=edge_out.at[i], dst_ref=edge_in.at[i], send_sem=edge_send.at[i], recv_sem=edge_recv.at[i],
            device_id=following, device_id_type=MESH,
        )
        for i in range(3)
    ]
    inside = jnp.where(me == 0, 0.0, 1.0)
    for h in range(HALVES):
        parts = [part for both in zip(last_rows(kbuf, h), last_rows(vbuf, h)) for part in both]
        edge_out[h] = jnp.concatenate(parts, axis=0).astype(BF16)

    def lanes_of(owner, h):
        return pl.ds(pl.multiple_of((HALVES * owner + h) * LANES, LANES), LANES)

    def block_lanes(owner):
        return pl.ds(pl.multiple_of(owner * LANES, LANES), LANES)

    def tap_rows(which, lanes):
        return [taps[which, i : i + 1, lanes] for i in range(3)]

    def gate(rows, owner, h):
        lanes = lanes_of(owner, h)
        if rows == 16:
            before = [edges[h, i : i + 1, block_lanes(owner)] for i in range(4)]
        else:
            before = [jnp.zeros((1, LANES), F32)] * 4
        fk = featurize(kbuf[:rows, lanes].astype(F32), tap_rows(1, lanes), before[0], before[1])
        fv = featurize(vbuf[:rows, lanes].astype(F32), tap_rows(2, lanes), before[2], before[3])
        return (fk * fv).astype(BF16)

    def copy_to(src, dst, send, recv, to, h, origin):
        return pltpu.make_async_remote_copy(
            src_ref=src.at[h, to], dst_ref=dst.at[h, origin], send_sem=send.at[h, to], recv_sem=recv.at[h, origin],
            device_id={"ctx": to}, device_id_type=MESH,
        )

    def to_channels(h, to, origin):
        return copy_to(gated, moved, send_one, recv_one, to, h, origin)

    def to_positions(h, to, origin):
        return copy_to(conv, back, send_two, recv_two, to, h, origin)

    def gate_rest(h):
        def one(owner, carry):
            gated[h, owner, 16:] = gate(ROWS, owner, h)[16:]
            return carry

        lax.fori_loop(0, BLOCKS, one, 0)

    def gate_top(h):
        arrived = edge_in[h].astype(F32) * inside
        for s in range(4):
            edges[h, 0:4, 1024 * s : 1024 * s + 1024] = arrived[4 * s : 4 * s + 4]

        def one(owner, carry):
            gated[h, owner, :16] = gate(16, owner, h)
            return carry

        lax.fori_loop(0, BLOCKS, one, 0)

    gate_rest(0)
    pl.semaphore_wait(barrier, BLOCKS - 1)
    for h in range(HALVES):
        edge_copies[h].start()
    loads[5].start()
    loads[6].start()
    def send_gated(h):
        for offset in offsets():
            to_channels(h, at(offset), me).start()
        moved[h, me] = gated[h, me]

    edge_copies[0].wait_recv()
    gate_top(0)
    send_gated(0)
    gate_rest(1)
    edge_copies[1].wait_recv()
    gate_top(1)

    for i in (4, 5, 6):
        loads[i].wait()

    def filter_outer(g):
        turned = []
        for i in range(2):
            rows = pl.ds(pl.multiple_of(16 * g + 8 * i, 8), 8)
            top, low = split(fbuf[:, rows, :].reshape(8 * BLOCKS, HALVES * LANES))
            part = dot(t_outer[0], top) + dot(t_outer[1], top) + dot(t_outer[0], low)
            turned.append(part.reshape(2 * BLOCKS, 8, HALVES * LANES))
        top, low = split(jnp.concatenate(turned, axis=1))
        rows = pl.ds(pl.multiple_of(16 * g, 16), 16)
        spec[:, rows, :] = top
        spec_low[:, rows, :] = low

    loop(8, 2, filter_outer)
    for i in (7, 8, 9, 3):
        loads[i].start()
    send_gated(1)

    def filter_inner(k):
        slot = pl.ds(pl.multiple_of(2 * k, 2), 2)
        top = spec[slot].reshape(2 * ROWS, HALVES * LANES)
        low = spec_low[slot].reshape(2 * ROWS, HALVES * LANES)
        fspec[k] = dot(t_inner[0, k], top) + dot(t_inner[1, k], top) + dot(t_inner[0, k], low)

    loop(BLOCKS, 8, filter_inner)

    loads[3].wait()
    edge_out[2] = jnp.concatenate([part for h in range(HALVES) for part in last_rows(qbuf, h)], axis=0).astype(BF16)
    edge_copies[2].start()
    for i in (7, 8, 9):
        loads[i].wait()

    def feature_q(owner, carry):
        for h in range(HALVES):
            lanes = lanes_of(owner, h)
            before = [edges[h, i : i + 1, block_lanes(owner)] for i in (4, 5)]
            fbuf[owner, :, h * LANES : (h + 1) * LANES] = featurize(
                qbuf[:, lanes].astype(F32), tap_rows(0, lanes), before[0], before[1]
            )
        return carry

    def convolve(h):
        half = pl.ds(h * LANES, LANES)
        first = pl.ds(0, LANES)

        def signal_outer(g):
            rows = pl.ds(pl.multiple_of(16 * g, 16), 16)
            pairs = side_by_side(moved[h, :, rows, :].astype(F32), BLOCKS).astype(BF16)
            spec[:, rows, first] = stacked(dot(t_outer[0], pairs), 2 * BLOCKS).astype(BF16)

        loop(8, 4, signal_outer)

        def signal_inner(k):
            slot = pl.ds(pl.multiple_of(2 * k, 2), 2)
            signal = dot(t_inner[0, k], spec[slot, :, first].reshape(2 * ROWS, LANES))
            real, imag = signal[:ROWS], signal[ROWS:]
            f_real, f_imag = fspec[k, :ROWS, half], fspec[k, ROWS:, half]
            lone = (lax.broadcasted_iota(jnp.int32, (ROWS, LANES), 0) == 0) & (k == 0)
            f_last = jnp.where(lone, f_imag, f_real)
            f_imag = jnp.where(lone, 0.0, f_imag)
            product = jnp.concatenate([real * f_real - imag * f_imag, real * f_imag + imag * f_last], axis=0)
            restored = dot(t_inner_back[k], product.astype(BF16)).astype(BF16)
            spec_low[slot, :, first] = restored.reshape(2, ROWS, LANES)

        loop(BLOCKS, 8, signal_inner)
        gain = sbuf[:, h * LANES : (h + 1) * LANES]

        def signal_back(g):
            rows = pl.ds(pl.multiple_of(16 * g, 16), 16)
            pairs = side_by_side(spec_low[:, rows, first].astype(F32), 2 * BLOCKS).astype(BF16)
            restored = stacked(dot(t_outer_back[...], pairs), BLOCKS)
            conv[h, :, rows, :] = (restored + gain * moved[h, :, rows, :].astype(F32)).astype(BF16)

        loop(8, 4, signal_back)

    for h in range(HALVES):
        def await_gated(j, carry):
            origin = (me + j) % BLOCKS
            to_channels(h, origin, origin).wait_recv()
            return carry

        lax.fori_loop(1, BLOCKS, await_gated, 0)
        convolve(h)
        for offset in offsets():
            to_positions(h, at(offset), me).start()
        back[h, me] = conv[h, me]

    edge_copies[2].wait_recv()
    arrived_q = edge_in[2].astype(F32) * inside
    for h in range(HALVES):
        for s in range(4):
            row = 8 * h + 2 * s
            edges[h, 4:6, 1024 * s : 1024 * s + 1024] = arrived_q[row : row + 2]
    lax.fori_loop(0, BLOCKS, feature_q, 0)

    def mix(h, origin):
        features = fbuf[origin, :, h * LANES : (h + 1) * LANES]
        out[:, lanes_of(origin, h)] = (features * back[h, origin].astype(F32)).astype(BF16)

    for h in range(HALVES):
        mix(h, me)
        for offset in offsets():
            origin = at(offset, -1)
            to_positions(h, origin, origin).wait_recv()
            mix(h, origin)

    for copy in edge_copies:
        copy.wait_send()

    def finish(j, carry):
        to = (me + j) % BLOCKS
        for h in range(HALVES):
            to_channels(h, to, me).wait_send()
            to_positions(h, to, me).wait_send()
        return carry

    lax.fori_loop(1, BLOCKS, finish, 0)


def on_device(query_rows, key_rows, value_rows, short_taps, long_filter, skip_gain):
    rows, width = query_rows.shape
    outer, inner, inner_back, outer_back = transform_tables()
    tables = [high_low(outer), high_low(inner), high(inner_back), high(outer_back)]
    any_spec = pl.BlockSpec(memory_space=pl.ANY)
    dma = pltpu.SemaphoreType.DMA
    blocks = (HALVES, BLOCKS, ROWS, LANES)
    return pl.pallas_call(
        kernel,
        out_shape=pltpu.VMEM((rows, width), BF16),
        in_specs=[any_spec] * 10,
        out_specs=pl.BlockSpec(memory_space=pltpu.VMEM),
        scratch_shapes=[
            pltpu.VMEM((rows, width), BF16), pltpu.VMEM((rows, width), BF16), pltpu.VMEM((rows, width), BF16),
            pltpu.VMEM((3, 3, width), F32), pltpu.VMEM((BLOCKS, ROWS, HALVES * LANES), F32), pltpu.VMEM((1, HALVES * LANES), F32),
            *[pltpu.VMEM(t.shape, BF16) for t in tables],
            pltpu.VMEM((3, 16, 1024), BF16), pltpu.VMEM((3, 16, 1024), BF16), pltpu.VMEM((HALVES, 8, width // HALVES), F32),
            *[pltpu.VMEM(blocks, BF16)] * 4,
            *[pltpu.VMEM((2 * BLOCKS, ROWS, HALVES * LANES), BF16)] * 2,
            pltpu.VMEM((BLOCKS, 2 * ROWS, HALVES * LANES), F32),
            dma((10,)), dma((3,)), dma((3,)), *[dma((HALVES, BLOCKS))] * 4,
        ],
        compiler_params=pltpu.CompilerParams(collective_id=0, has_side_effects=True, vmem_limit_bytes=56 << 20),
        name="mixer",
    )(
        query_rows, key_rows, value_rows, short_taps, long_filter.reshape(BLOCKS, ROWS, HALVES * LANES),
        skip_gain.reshape(1, HALVES * LANES), *[jnp.asarray(t) for t in tables],
    )


def solution(mesh):
    in_specs = (P(("dp", "ctx"), None), P(("dp", "ctx"), None), P(("dp", "ctx"), None), P(), P(None, "ctx"), P("ctx"))
    return jax.shard_map(on_device, mesh=mesh, in_specs=in_specs, out_specs=P(("dp", "ctx"), None), check_vma=False)
```

```python
import functools

import jax
import jax.numpy as jnp
import ml_dtypes
import numpy as np
from jax import lax
from jax.experimental import pallas as pl
from jax.experimental.pallas import tpu as pltpu
from jax.sharding import PartitionSpec as P

F32, BF16 = jnp.float32, jnp.bfloat16
MESH = pl.DeviceIdType.MESH

BLOCKS, ROWS, LANES = 32, 128, 128
FULL = 2 * BLOCKS * ROWS
HALVES = 2


def transform_tables():
    p, k1 = np.arange(BLOCKS), np.arange(BLOCKS)
    angle = 2 * np.pi * (k1[:, None] * p % 64) / 64
    outer = np.zeros((BLOCKS, 2, BLOCKS))
    outer[:, 0], outer[:, 1] = np.cos(angle), -np.sin(angle)
    outer[0, 1] = np.cos(np.pi * p)
    outer_back = np.zeros((BLOCKS, BLOCKS, 2))
    outer_back[:, :, 0], outer_back[:, :, 1] = 2 * np.cos(angle.T), -2 * np.sin(angle.T)
    outer_back[:, 0, 0], outer_back[:, 0, 1] = 1, np.cos(np.pi * p)
    outer_back /= FULL
    r, k2 = np.arange(ROWS), np.arange(ROWS)
    inner = np.zeros((BLOCKS + 1, ROWS, 2 * ROWS))
    inner_back = np.zeros((BLOCKS + 1, ROWS, 2 * ROWS))
    for k in range(1, BLOCKS):
        turn = 2 * np.pi * ((k + 64 * k2)[:, None] * r % FULL) / FULL
        inner[k] = np.block([np.cos(turn), np.sin(turn)])
        inner_back[k] = np.block([np.cos(turn.T), np.sin(turn.T)])
    half = np.arange(64)[:, None]
    even = 2 * np.pi * (64 * half * r % FULL) / FULL
    odd = 2 * np.pi * ((32 + 64 * half) * r % FULL) / FULL
    lone = np.zeros((2 * ROWS, 2 * ROWS))
    lone[0:64, :ROWS], lone[64:128, ROWS:] = np.cos(even), np.cos(odd)
    lone[128:192, :ROWS], lone[192:256, ROWS:] = -np.sin(even), -np.sin(odd)
    lone[128, :ROWS] = np.cos(np.pi * r)
    weight = np.full(2 * ROWS, 2.0)
    weight[0] = weight[128] = 1
    inner[0], inner[BLOCKS] = lone[:ROWS], lone[ROWS:]
    inner_back[0], inner_back[BLOCKS] = (lone.T * weight)[:ROWS], (lone.T * weight)[ROWS:]
    eye = np.eye(8)
    outer = np.kron(outer.reshape(2 * BLOCKS, BLOCKS), eye)
    outer_back = np.kron(outer_back.reshape(BLOCKS, 2 * BLOCKS), eye)
    return outer, inner, inner_back, outer_back


def high_low(table):
    table = table.astype(np.float32)
    high = table.astype(ml_dtypes.bfloat16)
    return np.stack([high, (table - high.astype(np.float32)).astype(ml_dtypes.bfloat16)])


def high(table):
    return table.astype(np.float32).astype(ml_dtypes.bfloat16)


def dot(a, b):
    return jnp.dot(a, b, preferred_element_type=F32)


def split(a):
    top = a.astype(BF16)
    return top, (a - top.astype(F32)).astype(BF16)


def side_by_side(x, n):
    return jnp.concatenate([x[:, :8].reshape(8 * n, LANES), x[:, 8:].reshape(8 * n, LANES)], axis=1)


def stacked(z, n):
    return jnp.concatenate([z[:, :LANES].reshape(n, 8, LANES), z[:, LANES:].reshape(n, 8, LANES)], axis=1)


def crossed(real, imag):
    return jnp.concatenate(
        [jnp.concatenate([real, imag], axis=1), jnp.concatenate([imag, -real], axis=1)], axis=0
    )


def slots(step, lone, body):
    lone()
    for k in range(1, step):
        body(k)

    def several(j, carry):
        for i in range(step):
            body(j * step + i)
        return carry

    lax.fori_loop(1, BLOCKS // step, several, 0)


def loop(count, step, body):
    def several(j, carry):
        for i in range(step):
            body(j * step + i)
        return carry

    lax.fori_loop(0, count // step, several, 0)


def featurize(block, taps, edge_two, edge_one):
    row = lax.broadcasted_iota(jnp.int32, (8, LANES), 0)
    one, two = pltpu.roll(block, 1, 0), pltpu.roll(block, 2, 0)
    top_one = jnp.where(row == 0, edge_one, one[:8])
    top_two = jnp.where(row == 0, edge_two, jnp.where(row == 1, edge_one, two[:8]))
    one = jnp.concatenate([top_one, one[8:]], axis=0)
    two = jnp.concatenate([top_two, two[8:]], axis=0)
    return taps[0] * block + taps[1] * one + taps[2] * two


def offsets():
    span = [(dx, dy, dz) for dy in range(4) for dz in range(2) for dx in range(4)]
    far = sorted(span, key=lambda o: -(min(o[0], 4 - o[0]) + min(o[1], 4 - o[1]) + o[2]))[:-1]
    return [far[j // 2] if j % 2 == 0 else far[-1 - j // 2] for j in range(31)]


def kernel(
    query, key, value, short_taps, filt, skip, outer, inner, inner_back, outer_back, out,
    qbuf, kbuf, vbuf, taps, fbuf, sbuf, t_outer, t_inner, t_inner_back, t_outer_back,
    edge_out, edge_in, edges, gated, moved, conv, back, spec, spec_low, fspec,
    load_sem, edge_send, edge_recv, send_one, recv_one, send_two, recv_two,
):
    me = lax.axis_index("ctx")
    x, z, y = me % 4, (me // 4) % 2, me // 8
    sign = 1 - 2 * (lax.axis_index("dp") % 2)

    def at(offset, way=1):
        dx, dy, dz = offset
        return ((y + 4 + way * sign * dy) % 4 * 2 + (z + dz) % 2) * 4 + (x + 4 + way * sign * dx) % 4

    barrier = pltpu.get_barrier_semaphore()

    def greet(j, carry):
        pl.semaphore_signal(barrier, inc=1, device_id={"ctx": (me + j) % BLOCKS}, device_id_type=MESH)
        return carry

    lax.fori_loop(1, BLOCKS, greet, 0)

    loads = [
        pltpu.make_async_copy(src, dst, load_sem.at[i])
        for i, (src, dst) in enumerate(
            [
                (key, kbuf), (value, vbuf), (short_taps, taps), (query, qbuf), (filt, fbuf), (outer, t_outer),
                (inner, t_inner), (skip, sbuf), (inner_back, t_inner_back), (outer_back, t_outer_back),
            ]
        )
    ]
    for i in (0, 1, 2):
        loads[i].start()
    for i in (0, 1, 2):
        loads[i].wait()
    loads[4].start()

    def last_rows(buf, h):
        rows = buf[ROWS - 16 :, :].astype(F32)[14:16]
        picked = [rows[:, (HALVES * b + h) * LANES : (HALVES * b + h + 1) * LANES] for b in range(BLOCKS)]
        return [jnp.concatenate(picked[8 * s : 8 * s + 8], axis=1) for s in range(4)]

    following = {"ctx": (me + 1) % BLOCKS}
    edge_copies = [
        pltpu.make_async_remote_copy(
            src_ref=edge_out.at[i], dst_ref=edge_in.at[i], send_sem=edge_send.at[i], recv_sem=edge_recv.at[i],
            device_id=following, device_id_type=MESH,
        )
        for i in range(3)
    ]
    inside = jnp.where(me == 0, 0.0, 1.0)
    for h in range(HALVES):
        parts = [part for both in zip(last_rows(kbuf, h), last_rows(vbuf, h)) for part in both]
        edge_out[h] = jnp.concatenate(parts, axis=0).astype(BF16)

    def lanes_of(owner, h):
        return pl.ds(pl.multiple_of((HALVES * owner + h) * LANES, LANES), LANES)

    def block_lanes(owner):
        return pl.ds(pl.multiple_of(owner * LANES, LANES), LANES)

    def tap_rows(which, lanes):
        return [taps[which, i : i + 1, lanes] for i in range(3)]

    def gate(rows, owner, h):
        lanes = lanes_of(owner, h)
        if rows == 16:
            before = [edges[h, i : i + 1, block_lanes(owner)] for i in range(4)]
        else:
            before = [jnp.zeros((1, LANES), F32)] * 4
        fk = featurize(kbuf[:rows, lanes].astype(F32), tap_rows(1, lanes), before[0], before[1])
        fv = featurize(vbuf[:rows, lanes].astype(F32), tap_rows(2, lanes), before[2], before[3])
        return (fk * fv).astype(BF16)

    def copy_to(src, dst, send, recv, to, h, origin):
        return pltpu.make_async_remote_copy(
            src_ref=src.at[h, to], dst_ref=dst.at[h, origin], send_sem=send.at[h, to], recv_sem=recv.at[h, origin],
            device_id={"ctx": to}, device_id_type=MESH,
        )

    def to_channels(h, to, origin):
        return copy_to(gated, moved, send_one, recv_one, to, h, origin)

    def to_positions(h, to, origin):
        return copy_to(conv, back, send_two, recv_two, to, h, origin)

    def gate_rest(h):
        def one(owner, carry):
            gated[h, owner, 16:] = gate(ROWS, owner, h)[16:]
            return carry

        lax.fori_loop(0, BLOCKS, one, 0)

    def gate_top(h):
        arrived = edge_in[h].astype(F32) * inside
        for s in range(4):
            edges[h, 0:4, 1024 * s : 1024 * s + 1024] = arrived[4 * s : 4 * s + 4]

        def one(owner, carry):
            gated[h, owner, :16] = gate(16, owner, h)
            return carry

        lax.fori_loop(0, BLOCKS, one, 0)

    gate_rest(0)
    pl.semaphore_wait(barrier, BLOCKS - 1)
    for h in range(HALVES):
        edge_copies[h].start()
    loads[5].start()
    loads[6].start()
    def send_gated(h):
        for offset in offsets():
            to_channels(h, at(offset), me).start()
        moved[h, me] = gated[h, me]

    edge_copies[0].wait_recv()
    gate_top(0)
    send_gated(0)
    gate_rest(1)
    edge_copies[1].wait_recv()
    gate_top(1)

    for i in (4, 5, 6):
        loads[i].wait()

    def filter_outer(g):
        turned = []
        for i in range(2):
            rows = pl.ds(pl.multiple_of(16 * g + 8 * i, 8), 8)
            top, low = split(fbuf[:, rows, :].reshape(8 * BLOCKS, HALVES * LANES))
            part = dot(t_outer[0], top) + dot(t_outer[1], top) + dot(t_outer[0], low)
            turned.append(part.reshape(2 * BLOCKS, 8, HALVES * LANES))
        top, low = split(jnp.concatenate(turned, axis=1))
        rows = pl.ds(pl.multiple_of(16 * g, 16), 16)
        spec[:, rows, :] = top
        spec_low[:, rows, :] = low

    loop(8, 2, filter_outer)
    for i in (7, 8, 9, 3):
        loads[i].start()
    send_gated(1)

    def filter_dot(k, top, low):
        return dot(t_inner[0, k], top) + dot(t_inner[1, k], top) + dot(t_inner[0, k], low)

    def filter_lone():
        top = spec[0:2].reshape(2 * ROWS, HALVES * LANES)
        low = spec_low[0:2].reshape(2 * ROWS, HALVES * LANES)
        fspec[0, :ROWS] = filter_dot(0, top, low)
        fspec[0, ROWS:] = filter_dot(BLOCKS, top, low)

    def filter_inner(k):
        both = filter_dot(
            k, crossed(spec[2 * k], spec[2 * k + 1]), crossed(spec_low[2 * k], spec_low[2 * k + 1])
        )
        fspec[k, :ROWS] = both[:, : HALVES * LANES]
        fspec[k, ROWS:] = both[:, HALVES * LANES :]

    slots(8, filter_lone, filter_inner)

    loads[3].wait()
    edge_out[2] = jnp.concatenate([part for h in range(HALVES) for part in last_rows(qbuf, h)], axis=0).astype(BF16)
    edge_copies[2].start()
    for i in (7, 8, 9):
        loads[i].wait()

    def feature_q(owner, carry):
        for h in range(HALVES):
            lanes = lanes_of(owner, h)
            before = [edges[h, i : i + 1, block_lanes(owner)] for i in (4, 5)]
            fbuf[owner, :, h * LANES : (h + 1) * LANES] = featurize(
                qbuf[:, lanes].astype(F32), tap_rows(0, lanes), before[0], before[1]
            )
        return carry

    def convolve(h):
        half = pl.ds(h * LANES, LANES)
        first = pl.ds(0, LANES)

        def signal_outer(g):
            rows = pl.ds(pl.multiple_of(16 * g, 16), 16)
            pairs = side_by_side(moved[h, :, rows, :].astype(F32), BLOCKS).astype(BF16)
            spec[:, rows, first] = stacked(dot(t_outer[0], pairs), 2 * BLOCKS).astype(BF16)

        loop(8, 8, signal_outer)

        def signal_lone():
            signal = spec[0:2, :, first].reshape(2 * ROWS, LANES)
            real, imag = dot(t_inner[0, 0], signal), dot(t_inner[0, BLOCKS], signal)
            f_real, f_imag = fspec[0, :ROWS, half], fspec[0, ROWS:, half]
            top = lax.broadcasted_iota(jnp.int32, (ROWS, LANES), 0) == 0
            f_last = jnp.where(top, f_imag, f_real)
            f_imag = jnp.where(top, 0.0, f_imag)
            product = jnp.concatenate([real * f_real - imag * f_imag, real * f_imag + imag * f_last], axis=0)
            product = product.astype(BF16)
            spec_low[0, :, first] = dot(t_inner_back[0], product).astype(BF16)
            spec_low[1, :, first] = dot(t_inner_back[BLOCKS], product).astype(BF16)

        def signal_inner(k):
            signal = dot(t_inner[0, k], crossed(spec[2 * k, :, first], spec[2 * k + 1, :, first]))
            real, imag = signal[:, :LANES], signal[:, LANES:]
            f_real, f_imag = fspec[k, :ROWS, half], fspec[k, ROWS:, half]
            up = (real * f_real - imag * f_imag).astype(BF16)
            across = (real * f_imag + imag * f_real).astype(BF16)
            restored = dot(t_inner_back[k], crossed(across, up)).astype(BF16)
            spec_low[2 * k, :, first] = restored[:, LANES:]
            spec_low[2 * k + 1, :, first] = restored[:, :LANES]

        slots(16, signal_lone, signal_inner)
        gain = sbuf[:, h * LANES : (h + 1) * LANES]

        def signal_back(g):
            rows = pl.ds(pl.multiple_of(16 * g, 16), 16)
            pairs = side_by_side(spec_low[:, rows, first].astype(F32), 2 * BLOCKS).astype(BF16)
            restored = stacked(dot(t_outer_back[...], pairs), BLOCKS)
            conv[h, :, rows, :] = (restored + gain * moved[h, :, rows, :].astype(F32)).astype(BF16)

        loop(8, 8, signal_back)

    for h in range(HALVES):
        def await_gated(j, carry):
            origin = (me + j) % BLOCKS
            to_channels(h, origin, origin).wait_recv()
            return carry

        lax.fori_loop(1, BLOCKS, await_gated, 0)
        convolve(h)
        for offset in offsets():
            to_positions(h, at(offset), me).start()
        back[h, me] = conv[h, me]

    edge_copies[2].wait_recv()
    arrived_q = edge_in[2].astype(F32) * inside
    for h in range(HALVES):
        for s in range(4):
            row = 8 * h + 2 * s
            edges[h, 4:6, 1024 * s : 1024 * s + 1024] = arrived_q[row : row + 2]
    lax.fori_loop(0, BLOCKS, feature_q, 0)

    def mix(h, origin):
        features = fbuf[origin, :, h * LANES : (h + 1) * LANES]
        out[:, lanes_of(origin, h)] = (features * back[h, origin].astype(F32)).astype(BF16)

    for h in range(HALVES):
        mix(h, me)
        for offset in offsets():
            origin = at(offset, -1)
            to_positions(h, origin, origin).wait_recv()
            mix(h, origin)

    for copy in edge_copies:
        copy.wait_send()

    def finish(j, carry):
        to = (me + j) % BLOCKS
        for h in range(HALVES):
            to_channels(h, to, me).wait_send()
            to_positions(h, to, me).wait_send()
        return carry

    lax.fori_loop(1, BLOCKS, finish, 0)


def on_device(query_rows, key_rows, value_rows, short_taps, long_filter, skip_gain):
    rows, width = query_rows.shape
    outer, inner, inner_back, outer_back = transform_tables()
    tables = [high_low(outer), high_low(inner), high(inner_back), high(outer_back)]
    any_spec = pl.BlockSpec(memory_space=pl.ANY)
    dma = pltpu.SemaphoreType.DMA
    blocks = (HALVES, BLOCKS, ROWS, LANES)
    return pl.pallas_call(
        kernel,
        out_shape=pltpu.VMEM((rows, width), BF16),
        in_specs=[any_spec] * 10,
        out_specs=pl.BlockSpec(memory_space=pltpu.VMEM),
        scratch_shapes=[
            pltpu.VMEM((rows, width), BF16), pltpu.VMEM((rows, width), BF16), pltpu.VMEM((rows, width), BF16),
            pltpu.VMEM((3, 3, width), F32), pltpu.VMEM((BLOCKS, ROWS, HALVES * LANES), F32), pltpu.VMEM((1, HALVES * LANES), F32),
            *[pltpu.VMEM(t.shape, BF16) for t in tables],
            pltpu.VMEM((3, 16, 1024), BF16), pltpu.VMEM((3, 16, 1024), BF16), pltpu.VMEM((HALVES, 8, width // HALVES), F32),
            *[pltpu.VMEM(blocks, BF16)] * 4,
            *[pltpu.VMEM((2 * BLOCKS, ROWS, HALVES * LANES), BF16)] * 2,
            pltpu.VMEM((BLOCKS, 2 * ROWS, HALVES * LANES), F32),
            dma((10,)), dma((3,)), dma((3,)), *[dma((HALVES, BLOCKS))] * 4,
        ],
        compiler_params=pltpu.CompilerParams(collective_id=0, has_side_effects=True, vmem_limit_bytes=56 << 20),
        name="mixer",
    )(
        query_rows, key_rows, value_rows, short_taps, long_filter.reshape(BLOCKS, ROWS, HALVES * LANES),
        skip_gain.reshape(1, HALVES * LANES), *[jnp.asarray(t) for t in tables],
    )


def solution(mesh):
    in_specs = (P(("dp", "ctx"), None), P(("dp", "ctx"), None), P(("dp", "ctx"), None), P(), P(None, "ctx"), P("ctx"))
    return jax.shard_map(on_device, mesh=mesh, in_specs=in_specs, out_specs=P(("dp", "ctx"), None), check_vma=False)
```

```python
import functools

import jax
import jax.numpy as jnp
import ml_dtypes
import numpy as np
from jax import lax
from jax.experimental import pallas as pl
from jax.experimental.pallas import tpu as pltpu
from jax.sharding import PartitionSpec as P

F32, BF16 = jnp.float32, jnp.bfloat16
MESH = pl.DeviceIdType.MESH

BLOCKS, ROWS, LANES = 32, 128, 128
FULL = 2 * BLOCKS * ROWS
HALVES = 2


def transform_tables():
    p, k1 = np.arange(BLOCKS), np.arange(BLOCKS)
    angle = 2 * np.pi * (k1[:, None] * p % 64) / 64
    outer = np.zeros((BLOCKS, 2, BLOCKS))
    outer[:, 0], outer[:, 1] = np.cos(angle), -np.sin(angle)
    outer[0, 1] = np.cos(np.pi * p)
    outer_back = np.zeros((BLOCKS, BLOCKS, 2))
    outer_back[:, :, 0], outer_back[:, :, 1] = 2 * np.cos(angle.T), -2 * np.sin(angle.T)
    outer_back[:, 0, 0], outer_back[:, 0, 1] = 1, np.cos(np.pi * p)
    outer_back /= FULL
    r, k2 = np.arange(ROWS), np.arange(ROWS)
    inner = np.zeros((BLOCKS + 1, ROWS, 2 * ROWS))
    inner_back = np.zeros((BLOCKS + 1, ROWS, 2 * ROWS))
    for k in range(1, BLOCKS):
        turn = 2 * np.pi * ((k + 64 * k2)[:, None] * r % FULL) / FULL
        inner[k] = np.block([np.cos(turn), np.sin(turn)])
        inner_back[k] = np.block([np.cos(turn.T), np.sin(turn.T)])
    half = np.arange(64)[:, None]
    even = 2 * np.pi * (64 * half * r % FULL) / FULL
    odd = 2 * np.pi * ((32 + 64 * half) * r % FULL) / FULL
    lone = np.zeros((2 * ROWS, 2 * ROWS))
    lone[0:64, :ROWS], lone[64:128, ROWS:] = np.cos(even), np.cos(odd)
    lone[128:192, :ROWS], lone[192:256, ROWS:] = -np.sin(even), -np.sin(odd)
    lone[128, :ROWS] = np.cos(np.pi * r)
    weight = np.full(2 * ROWS, 2.0)
    weight[0] = weight[128] = 1
    inner[0], inner[BLOCKS] = lone[:ROWS], lone[ROWS:]
    inner_back[0], inner_back[BLOCKS] = (lone.T * weight)[:ROWS], (lone.T * weight)[ROWS:]
    eye = np.eye(8)
    outer = np.kron(outer.reshape(2 * BLOCKS, BLOCKS), eye)
    outer_back = np.kron(outer_back.reshape(BLOCKS, 2 * BLOCKS), eye)
    return outer, inner, inner_back, outer_back


def high_low(table):
    table = table.astype(np.float32)
    high = table.astype(ml_dtypes.bfloat16)
    return np.stack([high, (table - high.astype(np.float32)).astype(ml_dtypes.bfloat16)])


def high(table):
    return table.astype(np.float32).astype(ml_dtypes.bfloat16)


def dot(a, b):
    return jnp.dot(a, b, preferred_element_type=F32)


def split(a):
    top = a.astype(BF16)
    return top, (a - top.astype(F32)).astype(BF16)


def side_by_side(x, n):
    return jnp.concatenate([x[:, :8].reshape(8 * n, LANES), x[:, 8:].reshape(8 * n, LANES)], axis=1)


def stacked(z, n):
    return jnp.concatenate([z[:, :LANES].reshape(n, 8, LANES), z[:, LANES:].reshape(n, 8, LANES)], axis=1)


def crossed(real, imag):
    return jnp.concatenate(
        [jnp.concatenate([real, imag], axis=1), jnp.concatenate([imag, -real], axis=1)], axis=0
    )


def slots(step, lone, body):
    lone()
    for k in range(1, step):
        body(k)

    def several(j, carry):
        for i in range(step):
            body(j * step + i)
        return carry

    lax.fori_loop(1, BLOCKS // step, several, 0)


def loop(count, step, body):
    def several(j, carry):
        for i in range(step):
            body(j * step + i)
        return carry

    lax.fori_loop(0, count // step, several, 0)


def featurize(block, taps, edge_two, edge_one):
    row = lax.broadcasted_iota(jnp.int32, (8, LANES), 0)
    one, two = pltpu.roll(block, 1, 0), pltpu.roll(block, 2, 0)
    top_one = jnp.where(row == 0, edge_one, one[:8])
    top_two = jnp.where(row == 0, edge_two, jnp.where(row == 1, edge_one, two[:8]))
    one = jnp.concatenate([top_one, one[8:]], axis=0)
    two = jnp.concatenate([top_two, two[8:]], axis=0)
    return taps[0] * block + taps[1] * one + taps[2] * two


def offsets():
    def hops(o):
        return min(o[0], 4 - o[0]), min(o[1], 4 - o[1]), o[2]

    span = [(dx, dy, dz) for dy in range(4) for dz in range(2) for dx in range(4)]
    left = sorted(span, key=lambda o: -sum(hops(o)))[:-1]
    order = []
    while left:
        order.append(left.pop(0))
        along = hops(order[-1])
        rest = [o for o in left if hops(o) == (2 - along[0], 2 - along[1], 1 - along[2])]
        if rest:
            left.remove(rest[0])
            order.append(rest[0])
    return order


EARLY = 16


def kernel(
    query, key, value, short_taps, filt, skip, outer, inner, inner_back, outer_back, out,
    qbuf, kbuf, vbuf, taps, fbuf, sbuf, t_outer, t_inner, t_inner_back, t_outer_back,
    edge_out, edge_in, edges, gated, moved, conv, back, spec, spec_low, fspec,
    load_sem, edge_send, edge_recv, send_one, recv_one, send_top, recv_top, send_two, recv_two,
):
    me = lax.axis_index("ctx")
    x, z, y = me % 4, (me // 4) % 2, me // 8
    sign = 1 - 2 * (lax.axis_index("dp") % 2)

    def at(offset, way=1):
        dx, dy, dz = offset
        return ((y + 4 + way * sign * dy) % 4 * 2 + (z + dz) % 2) * 4 + (x + 4 + way * sign * dx) % 4

    loads = [
        pltpu.make_async_copy(src, dst, load_sem.at[i])
        for i, (src, dst) in enumerate(
            [
                (key, kbuf), (value, vbuf), (short_taps, taps), (query, qbuf), (filt, fbuf), (outer, t_outer),
                (inner, t_inner), (skip, sbuf), (inner_back, t_inner_back), (outer_back, t_outer_back),
            ]
        )
    ]
    for i in (0, 1, 2):
        loads[i].start()

    barrier = pltpu.get_barrier_semaphore()

    def greet(j, carry):
        pl.semaphore_signal(barrier, inc=1, device_id={"ctx": (me + j) % BLOCKS}, device_id_type=MESH)
        return carry

    lax.fori_loop(1, BLOCKS, greet, 0)
    for i in (0, 1, 2):
        loads[i].wait()
    loads[4].start()

    def last_rows(buf, h):
        rows = buf[ROWS - 16 :, :].astype(F32)[14:16]
        picked = [rows[:, (HALVES * b + h) * LANES : (HALVES * b + h + 1) * LANES] for b in range(BLOCKS)]
        return [jnp.concatenate(picked[8 * s : 8 * s + 8], axis=1) for s in range(4)]

    following = {"ctx": (me + 1) % BLOCKS}
    edge_copies = [
        pltpu.make_async_remote_copy(
            src_ref=edge_out.at[i], dst_ref=edge_in.at[i], send_sem=edge_send.at[i], recv_sem=edge_recv.at[i],
            device_id=following, device_id_type=MESH,
        )
        for i in range(3)
    ]
    inside = jnp.where(me == 0, 0.0, 1.0)
    for h in range(HALVES):
        parts = [part for both in zip(last_rows(kbuf, h), last_rows(vbuf, h)) for part in both]
        edge_out[h] = jnp.concatenate(parts, axis=0).astype(BF16)

    def lanes_of(owner, h):
        return pl.ds(pl.multiple_of((HALVES * owner + h) * LANES, LANES), LANES)

    def block_lanes(owner):
        return pl.ds(pl.multiple_of(owner * LANES, LANES), LANES)

    def tap_rows(which, lanes):
        return [taps[which, i : i + 1, lanes] for i in range(3)]

    def gate(rows, owner, h):
        lanes = lanes_of(owner, h)
        if rows == 16:
            before = [edges[h, i : i + 1, block_lanes(owner)] for i in range(4)]
        else:
            before = [jnp.zeros((1, LANES), F32)] * 4
        fk = featurize(kbuf[:rows, lanes].astype(F32), tap_rows(1, lanes), before[0], before[1])
        fv = featurize(vbuf[:rows, lanes].astype(F32), tap_rows(2, lanes), before[2], before[3])
        return (fk * fv).astype(BF16)

    def copy_to(src, dst, send, recv, to, h, origin):
        return pltpu.make_async_remote_copy(
            src_ref=src.at[h, to], dst_ref=dst.at[h, origin], send_sem=send.at[h, to], recv_sem=recv.at[h, origin],
            device_id={"ctx": to}, device_id_type=MESH,
        )

    def to_channels(h, to, origin):
        return copy_to(gated, moved, send_one, recv_one, to, h, origin)

    def part_to_channels(rows, send, recv, to, origin):
        return pltpu.make_async_remote_copy(
            src_ref=gated.at[0, to, rows], dst_ref=moved.at[0, origin, rows], send_sem=send, recv_sem=recv,
            device_id={"ctx": to}, device_id_type=MESH,
        )

    def rest_to_channels(to, origin):
        return part_to_channels(pl.ds(16, ROWS - 16), send_one.at[0, to], recv_one.at[0, origin], to, origin)

    def top_to_channels(to, origin):
        return part_to_channels(pl.ds(0, 16), send_top.at[to], recv_top.at[origin], to, origin)

    def first_half(j, to, origin):
        if j < EARLY:
            return [rest_to_channels(to, origin), top_to_channels(to, origin)]
        return [to_channels(0, to, origin)]

    def to_positions(h, to, origin):
        return copy_to(conv, back, send_two, recv_two, to, h, origin)

    def gate_rest(h):
        def one(owner, carry):
            gated[h, owner, 16:] = gate(ROWS, owner, h)[16:]
            return carry

        lax.fori_loop(0, BLOCKS, one, 0)

    def gate_top(h):
        arrived = edge_in[h].astype(F32) * inside
        for s in range(4):
            edges[h, 0:4, 1024 * s : 1024 * s + 1024] = arrived[4 * s : 4 * s + 4]

        def one(owner, carry):
            gated[h, owner, :16] = gate(16, owner, h)
            return carry

        lax.fori_loop(0, BLOCKS, one, 0)

    gate_rest(0)
    pl.semaphore_wait(barrier, BLOCKS - 1)
    for h in range(HALVES):
        edge_copies[h].start()
    loads[5].start()
    loads[6].start()
    for offset in offsets()[:EARLY]:
        rest_to_channels(at(offset), me).start()
    edge_copies[0].wait_recv()
    gate_top(0)
    for j, offset in enumerate(offsets()):
        first_half(j, at(offset), me)[-1].start()
    moved[0, me] = gated[0, me]
    gate_rest(1)
    edge_copies[1].wait_recv()
    gate_top(1)

    for i in (4, 5, 6):
        loads[i].wait()

    def filter_outer(g):
        turned = []
        for i in range(2):
            rows = pl.ds(pl.multiple_of(16 * g + 8 * i, 8), 8)
            top, low = split(fbuf[:, rows, :].reshape(8 * BLOCKS, HALVES * LANES))
            part = dot(t_outer[0], top) + dot(t_outer[1], top) + dot(t_outer[0], low)
            turned.append(part.reshape(2 * BLOCKS, 8, HALVES * LANES))
        top, low = split(jnp.concatenate(turned, axis=1))
        rows = pl.ds(pl.multiple_of(16 * g, 16), 16)
        spec[:, rows, :] = top
        spec_low[:, rows, :] = low

    loop(8, 2, filter_outer)
    for i in (7, 8, 9, 3):
        loads[i].start()
    for offset in offsets():
        to_channels(1, at(offset), me).start()
    moved[1, me] = gated[1, me]

    def filter_dot(k, top, low):
        return dot(t_inner[0, k], top) + dot(t_inner[1, k], top) + dot(t_inner[0, k], low)

    def filter_lone():
        top = spec[0:2].reshape(2 * ROWS, HALVES * LANES)
        low = spec_low[0:2].reshape(2 * ROWS, HALVES * LANES)
        fspec[0, :ROWS] = filter_dot(0, top, low)
        fspec[0, ROWS:] = filter_dot(BLOCKS, top, low)

    def filter_inner(k):
        both = filter_dot(
            k, crossed(spec[2 * k], spec[2 * k + 1]), crossed(spec_low[2 * k], spec_low[2 * k + 1])
        )
        fspec[k, :ROWS] = both[:, : HALVES * LANES]
        fspec[k, ROWS:] = both[:, HALVES * LANES :]

    slots(8, filter_lone, filter_inner)

    loads[3].wait()
    edge_out[2] = jnp.concatenate([part for h in range(HALVES) for part in last_rows(qbuf, h)], axis=0).astype(BF16)
    edge_copies[2].start()
    for i in (7, 8, 9):
        loads[i].wait()

    def feature_q(owner, carry):
        for h in range(HALVES):
            lanes = lanes_of(owner, h)
            before = [edges[h, i : i + 1, block_lanes(owner)] for i in (4, 5)]
            fbuf[owner, :, h * LANES : (h + 1) * LANES] = featurize(
                qbuf[:, lanes].astype(F32), tap_rows(0, lanes), before[0], before[1]
            )
        return carry

    def convolve(h):
        half = pl.ds(h * LANES, LANES)
        first = pl.ds(0, LANES)

        def signal_outer(g):
            rows = pl.ds(pl.multiple_of(16 * g, 16), 16)
            pairs = side_by_side(moved[h, :, rows, :].astype(F32), BLOCKS).astype(BF16)
            spec[:, rows, first] = stacked(dot(t_outer[0], pairs), 2 * BLOCKS).astype(BF16)

        loop(8, 8, signal_outer)

        def signal_lone():
            signal = spec[0:2, :, first].reshape(2 * ROWS, LANES)
            real, imag = dot(t_inner[0, 0], signal), dot(t_inner[0, BLOCKS], signal)
            f_real, f_imag = fspec[0, :ROWS, half], fspec[0, ROWS:, half]
            top = lax.broadcasted_iota(jnp.int32, (ROWS, LANES), 0) == 0
            f_last = jnp.where(top, f_imag, f_real)
            f_imag = jnp.where(top, 0.0, f_imag)
            product = jnp.concatenate([real * f_real - imag * f_imag, real * f_imag + imag * f_last], axis=0)
            product = product.astype(BF16)
            spec_low[0, :, first] = dot(t_inner_back[0], product).astype(BF16)
            spec_low[1, :, first] = dot(t_inner_back[BLOCKS], product).astype(BF16)

        def signal_inner(k):
            signal = dot(t_inner[0, k], crossed(spec[2 * k, :, first], spec[2 * k + 1, :, first]))
            real, imag = signal[:, :LANES], signal[:, LANES:]
            f_real, f_imag = fspec[k, :ROWS, half], fspec[k, ROWS:, half]
            up = (real * f_real - imag * f_imag).astype(BF16)
            across = (real * f_imag + imag * f_real).astype(BF16)
            restored = dot(t_inner_back[k], crossed(across, up)).astype(BF16)
            spec_low[2 * k, :, first] = restored[:, LANES:]
            spec_low[2 * k + 1, :, first] = restored[:, :LANES]

        slots(16, signal_lone, signal_inner)
        gain = sbuf[:, h * LANES : (h + 1) * LANES]

        def signal_back(g):
            rows = pl.ds(pl.multiple_of(16 * g, 16), 16)
            pairs = side_by_side(spec_low[:, rows, first].astype(F32), 2 * BLOCKS).astype(BF16)
            restored = stacked(dot(t_outer_back[...], pairs), BLOCKS)
            conv[h, :, rows, :] = (restored + gain * moved[h, :, rows, :].astype(F32)).astype(BF16)

        loop(8, 8, signal_back)

    for h in range(HALVES):
        for j, offset in enumerate(offsets()):
            origin = at(offset, -1)
            for copy in first_half(j, origin, origin) if h == 0 else [to_channels(1, origin, origin)]:
                copy.wait_recv()
        convolve(h)
        for offset in offsets():
            to_positions(h, at(offset), me).start()
        back[h, me] = conv[h, me]

    edge_copies[2].wait_recv()
    arrived_q = edge_in[2].astype(F32) * inside
    for h in range(HALVES):
        for s in range(4):
            row = 8 * h + 2 * s
            edges[h, 4:6, 1024 * s : 1024 * s + 1024] = arrived_q[row : row + 2]
    lax.fori_loop(0, BLOCKS, feature_q, 0)

    for j, offset in enumerate(offsets()):
        for copy in first_half(j, at(offset), me) + [to_channels(1, at(offset), me)]:
            copy.wait_send()
    for copy in edge_copies:
        copy.wait_send()

    def mix(h, origin):
        features = fbuf[origin, :, h * LANES : (h + 1) * LANES]
        out[:, lanes_of(origin, h)] = (features * back[h, origin].astype(F32)).astype(BF16)

    for h in range(HALVES):
        mix(h, me)
        for offset in offsets():
            origin = at(offset, -1)
            to_positions(h, origin, origin).wait_recv()
            mix(h, origin)
        for offset in offsets():
            to_positions(h, at(offset), me).wait_send()


def on_device(query_rows, key_rows, value_rows, short_taps, long_filter, skip_gain):
    rows, width = query_rows.shape
    outer, inner, inner_back, outer_back = transform_tables()
    tables = [high_low(outer), high_low(inner), high(inner_back), high(outer_back)]
    any_spec = pl.BlockSpec(memory_space=pl.ANY)
    dma = pltpu.SemaphoreType.DMA
    blocks = (HALVES, BLOCKS, ROWS, LANES)
    return pl.pallas_call(
        kernel,
        out_shape=pltpu.VMEM((rows, width), BF16),
        in_specs=[any_spec] * 10,
        out_specs=pl.BlockSpec(memory_space=pltpu.VMEM),
        scratch_shapes=[
            pltpu.VMEM((rows, width), BF16), pltpu.VMEM((rows, width), BF16), pltpu.VMEM((rows, width), BF16),
            pltpu.VMEM((3, 3, width), F32), pltpu.VMEM((BLOCKS, ROWS, HALVES * LANES), F32), pltpu.VMEM((1, HALVES * LANES), F32),
            *[pltpu.VMEM(t.shape, BF16) for t in tables],
            pltpu.VMEM((3, 16, 1024), BF16), pltpu.VMEM((3, 16, 1024), BF16), pltpu.VMEM((HALVES, 8, width // HALVES), F32),
            *[pltpu.VMEM(blocks, BF16)] * 4,
            *[pltpu.VMEM((2 * BLOCKS, ROWS, HALVES * LANES), BF16)] * 2,
            pltpu.VMEM((BLOCKS, 2 * ROWS, HALVES * LANES), F32),
            dma((10,)), dma((3,)), dma((3,)), *[dma((HALVES, BLOCKS))] * 2, *[dma((BLOCKS,))] * 2, *[dma((HALVES, BLOCKS))] * 2,
        ],
        compiler_params=pltpu.CompilerParams(collective_id=0, has_side_effects=True, vmem_limit_bytes=56 << 20),
        name="mixer",
    )(
        query_rows, key_rows, value_rows, short_taps, long_filter.reshape(BLOCKS, ROWS, HALVES * LANES),
        skip_gain.reshape(1, HALVES * LANES), *[jnp.asarray(t) for t in tables],
    )


def solution(mesh):
    in_specs = (P(("dp", "ctx"), None), P(("dp", "ctx"), None), P(("dp", "ctx"), None), P(), P(None, "ctx"), P("ctx"))
    return jax.shard_map(on_device, mesh=mesh, in_specs=in_specs, out_specs=P(("dp", "ctx"), None), check_vma=False)
```

```python
import functools

import jax
import jax.numpy as jnp
import ml_dtypes
import numpy as np
from jax import lax
from jax.experimental import pallas as pl
from jax.experimental.pallas import tpu as pltpu
from jax.sharding import PartitionSpec as P

F32, BF16 = jnp.float32, jnp.bfloat16
MESH = pl.DeviceIdType.MESH

BLOCKS, ROWS, LANES = 32, 128, 128
FULL = 2 * BLOCKS * ROWS
HALVES = 2


def transform_tables():
    p, k1 = np.arange(BLOCKS), np.arange(BLOCKS)
    angle = 2 * np.pi * (k1[:, None] * p % 64) / 64
    outer = np.zeros((BLOCKS, 2, BLOCKS))
    outer[:, 0], outer[:, 1] = np.cos(angle), -np.sin(angle)
    outer[0, 1] = np.cos(np.pi * p)
    outer_back = np.zeros((BLOCKS, BLOCKS, 2))
    outer_back[:, :, 0], outer_back[:, :, 1] = 2 * np.cos(angle.T), -2 * np.sin(angle.T)
    outer_back[:, 0, 0], outer_back[:, 0, 1] = 1, np.cos(np.pi * p)
    outer_back /= FULL
    r, k2 = np.arange(ROWS), np.arange(ROWS)
    inner = np.zeros((BLOCKS + 1, ROWS, 2 * ROWS))
    inner_back = np.zeros((BLOCKS + 1, ROWS, 2 * ROWS))
    for k in range(1, BLOCKS):
        turn = 2 * np.pi * ((k + 64 * k2)[:, None] * r % FULL) / FULL
        inner[k] = np.block([np.cos(turn), np.sin(turn)])
        inner_back[k] = np.block([np.cos(turn.T), np.sin(turn.T)])
    half = np.arange(64)[:, None]
    even = 2 * np.pi * (64 * half * r % FULL) / FULL
    odd = 2 * np.pi * ((32 + 64 * half) * r % FULL) / FULL
    lone = np.zeros((2 * ROWS, 2 * ROWS))
    lone[0:64, :ROWS], lone[64:128, ROWS:] = np.cos(even), np.cos(odd)
    lone[128:192, :ROWS], lone[192:256, ROWS:] = -np.sin(even), -np.sin(odd)
    lone[128, :ROWS] = np.cos(np.pi * r)
    weight = np.full(2 * ROWS, 2.0)
    weight[0] = weight[128] = 1
    inner[0], inner[BLOCKS] = lone[:ROWS], lone[ROWS:]
    inner_back[0], inner_back[BLOCKS] = (lone.T * weight)[:ROWS], (lone.T * weight)[ROWS:]
    eye = np.eye(8)
    outer = np.kron(outer.reshape(2 * BLOCKS, BLOCKS), eye)
    outer_back = np.kron(outer_back.reshape(BLOCKS, 2 * BLOCKS), eye)
    return outer, inner, inner_back, outer_back


def high_low(table):
    table = table.astype(np.float32)
    high = table.astype(ml_dtypes.bfloat16)
    return np.stack([high, (table - high.astype(np.float32)).astype(ml_dtypes.bfloat16)])


def high(table):
    return table.astype(np.float32).astype(ml_dtypes.bfloat16)


def dot(a, b):
    return jnp.dot(a, b, preferred_element_type=F32)


def split(a):
    top = a.astype(BF16)
    return top, (a - top.astype(F32)).astype(BF16)


def side_by_side(x, n):
    return jnp.concatenate([x[:, :8].reshape(8 * n, LANES), x[:, 8:].reshape(8 * n, LANES)], axis=1)


def stacked(z, n):
    return jnp.concatenate([z[:, :LANES].reshape(n, 8, LANES), z[:, LANES:].reshape(n, 8, LANES)], axis=1)


def crossed(real, imag):
    return jnp.concatenate(
        [jnp.concatenate([real, imag], axis=1), jnp.concatenate([imag, -real], axis=1)], axis=0
    )


def slots(step, lone, body):
    lone()
    for k in range(1, step):
        body(k)

    def several(j, carry):
        for i in range(step):
            body(j * step + i)
        return carry

    lax.fori_loop(1, BLOCKS // step, several, 0)


def loop(count, step, body):
    def several(j, carry):
        for i in range(step):
            body(j * step + i)
        return carry

    lax.fori_loop(0, count // step, several, 0)


def featurize(block, taps, edge_two, edge_one):
    row = lax.broadcasted_iota(jnp.int32, (8, LANES), 0)
    one, two = pltpu.roll(block, 1, 0), pltpu.roll(block, 2, 0)
    top_one = jnp.where(row == 0, edge_one, one[:8])
    top_two = jnp.where(row == 0, edge_two, jnp.where(row == 1, edge_one, two[:8]))
    one = jnp.concatenate([top_one, one[8:]], axis=0)
    two = jnp.concatenate([top_two, two[8:]], axis=0)
    return taps[0] * block + taps[1] * one + taps[2] * two


def offsets():
    def hops(o):
        return min(o[0], 4 - o[0]), min(o[1], 4 - o[1]), o[2]

    span = [(dx, dy, dz) for dy in range(4) for dz in range(2) for dx in range(4)]
    left = sorted(span, key=lambda o: -sum(hops(o)))[:-1]
    order = []
    while left:
        order.append(left.pop(0))
        along = hops(order[-1])
        rest = [o for o in left if hops(o) == (2 - along[0], 2 - along[1], 1 - along[2])]
        if rest:
            left.remove(rest[0])
            order.append(rest[0])
    return order


EARLY = 16


def kernel(
    query, key, value, short_taps, filt, skip, outer, inner, inner_back, outer_back, out,
    qbuf, kbuf, vbuf, taps, fbuf, sbuf, t_outer, t_inner, t_inner_back, t_outer_back,
    edge_out, edge_in, edges, gated, moved, conv, back, spec, spec_low, fspec,
    load_sem, edge_send, edge_recv, send_one, recv_one, send_top, recv_top, send_two, recv_two,
):
    me = lax.axis_index("ctx")
    x, z, y = me % 4, (me // 4) % 2, me // 8
    sign = 1 - 2 * (lax.axis_index("dp") % 2)

    def at(offset, way=1):
        dx, dy, dz = offset
        return ((y + 4 + way * sign * dy) % 4 * 2 + (z + dz) % 2) * 4 + (x + 4 + way * sign * dx) % 4

    ends = [
        pltpu.make_async_copy(src.at[pl.ds(ROWS - 16, 16)], dst.at[pl.ds(ROWS - 16, 16)], load_sem.at[10 + i])
        for i, (src, dst) in enumerate([(key, kbuf), (value, vbuf)])
    ]
    loads = [
        pltpu.make_async_copy(src, dst, load_sem.at[i])
        for i, (src, dst) in enumerate(
            [
                (key.at[pl.ds(0, ROWS - 16)], kbuf.at[pl.ds(0, ROWS - 16)]), (value.at[pl.ds(0, ROWS - 16)], vbuf.at[pl.ds(0, ROWS - 16)]), (short_taps, taps), (query, qbuf), (filt, fbuf), (outer, t_outer),
                (inner, t_inner), (skip, sbuf), (inner_back, t_inner_back), (outer_back, t_outer_back),
            ]
        )
    ]
    for load in ends:
        load.start()
    for i in (0, 1, 2):
        loads[i].start()

    barrier = pltpu.get_barrier_semaphore()

    def greet(j, carry):
        pl.semaphore_signal(barrier, inc=1, device_id={"ctx": (me + j) % BLOCKS}, device_id_type=MESH)
        return carry

    lax.fori_loop(1, BLOCKS, greet, 0)
    for load in ends:
        load.wait()

    def last_rows(buf, h):
        rows = buf[ROWS - 16 :, :].astype(F32)[14:16]
        picked = [rows[:, (HALVES * b + h) * LANES : (HALVES * b + h + 1) * LANES] for b in range(BLOCKS)]
        return [jnp.concatenate(picked[8 * s : 8 * s + 8], axis=1) for s in range(4)]

    following = {"ctx": (me + 1) % BLOCKS}
    edge_copies = [
        pltpu.make_async_remote_copy(
            src_ref=edge_out.at[i], dst_ref=edge_in.at[i], send_sem=edge_send.at[i], recv_sem=edge_recv.at[i],
            device_id=following, device_id_type=MESH,
        )
        for i in range(3)
    ]
    inside = jnp.where(me == 0, 0.0, 1.0)
    for h in range(HALVES):
        parts = [part for both in zip(last_rows(kbuf, h), last_rows(vbuf, h)) for part in both]
        edge_out[h] = jnp.concatenate(parts, axis=0).astype(BF16)

    def lanes_of(owner, h):
        return pl.ds(pl.multiple_of((HALVES * owner + h) * LANES, LANES), LANES)

    def block_lanes(owner):
        return pl.ds(pl.multiple_of(owner * LANES, LANES), LANES)

    def tap_rows(which, lanes):
        return [taps[which, i : i + 1, lanes] for i in range(3)]

    def gate(rows, owner, h):
        lanes = lanes_of(owner, h)
        if rows == 16:
            before = [edges[h, i : i + 1, block_lanes(owner)] for i in range(4)]
        else:
            before = [jnp.zeros((1, LANES), F32)] * 4
        fk = featurize(kbuf[:rows, lanes].astype(F32), tap_rows(1, lanes), before[0], before[1])
        fv = featurize(vbuf[:rows, lanes].astype(F32), tap_rows(2, lanes), before[2], before[3])
        return (fk * fv).astype(BF16)

    def copy_to(src, dst, send, recv, to, h, origin):
        return pltpu.make_async_remote_copy(
            src_ref=src.at[h, to], dst_ref=dst.at[h, origin], send_sem=send.at[h, to], recv_sem=recv.at[h, origin],
            device_id={"ctx": to}, device_id_type=MESH,
        )

    def to_channels(h, to, origin):
        return copy_to(gated, moved, send_one, recv_one, to, h, origin)

    def part_to_channels(rows, send, recv, to, origin):
        return pltpu.make_async_remote_copy(
            src_ref=gated.at[0, to, rows], dst_ref=moved.at[0, origin, rows], send_sem=send, recv_sem=recv,
            device_id={"ctx": to}, device_id_type=MESH,
        )

    def rest_to_channels(to, origin):
        return part_to_channels(pl.ds(16, ROWS - 16), send_one.at[0, to], recv_one.at[0, origin], to, origin)

    def top_to_channels(to, origin):
        return part_to_channels(pl.ds(0, 16), send_top.at[to], recv_top.at[origin], to, origin)

    def first_half(j, to, origin):
        if j < EARLY:
            return [rest_to_channels(to, origin), top_to_channels(to, origin)]
        return [to_channels(0, to, origin)]

    def to_positions(h, to, origin):
        return copy_to(conv, back, send_two, recv_two, to, h, origin)

    def gate_rest(h, owner):
        gated[h, owner, 16:] = gate(ROWS, owner, h)[16:]

    def gate_top(h):
        arrived = edge_in[h].astype(F32) * inside
        for s in range(4):
            edges[h, 0:4, 1024 * s : 1024 * s + 1024] = arrived[4 * s : 4 * s + 4]

        def one(owner, carry):
            gated[h, owner, :16] = gate(16, owner, h)
            return carry

        lax.fori_loop(0, BLOCKS, one, 0)

    for i in (0, 1, 2):
        loads[i].wait()
    pl.semaphore_wait(barrier, BLOCKS - 1)
    for h in range(HALVES):
        edge_copies[h].start()
    for offset in offsets()[:EARLY]:
        gate_rest(0, at(offset))
        rest_to_channels(at(offset), me).start()
    for i in (4, 5, 6):
        loads[i].start()
    for offset in offsets()[EARLY:]:
        gate_rest(0, at(offset))
    gate_rest(0, me)
    edge_copies[0].wait_recv()
    gate_top(0)
    for j, offset in enumerate(offsets()):
        first_half(j, at(offset), me)[-1].start()
    moved[0, me] = gated[0, me]

    def gate_second(owner, carry):
        gate_rest(1, owner)
        return carry

    lax.fori_loop(0, BLOCKS, gate_second, 0)
    edge_copies[1].wait_recv()
    gate_top(1)

    for i in (4, 5, 6):
        loads[i].wait()

    def filter_outer(g):
        turned = []
        for i in range(2):
            rows = pl.ds(pl.multiple_of(16 * g + 8 * i, 8), 8)
            top, low = split(fbuf[:, rows, :].reshape(8 * BLOCKS, HALVES * LANES))
            part = dot(t_outer[0], top) + dot(t_outer[1], top) + dot(t_outer[0], low)
            turned.append(part.reshape(2 * BLOCKS, 8, HALVES * LANES))
        top, low = split(jnp.concatenate(turned, axis=1))
        rows = pl.ds(pl.multiple_of(16 * g, 16), 16)
        spec[:, rows, :] = top
        spec_low[:, rows, :] = low

    loop(8, 2, filter_outer)
    for i in (7, 8, 9, 3):
        loads[i].start()
    for offset in offsets():
        to_channels(1, at(offset), me).start()
    moved[1, me] = gated[1, me]

    def filter_dot(k, top, low):
        return dot(t_inner[0, k], top) + dot(t_inner[1, k], top) + dot(t_inner[0, k], low)

    def filter_lone():
        top = spec[0:2].reshape(2 * ROWS, HALVES * LANES)
        low = spec_low[0:2].reshape(2 * ROWS, HALVES * LANES)
        fspec[0, :ROWS] = filter_dot(0, top, low)
        fspec[0, ROWS:] = filter_dot(BLOCKS, top, low)

    def filter_inner(k):
        both = filter_dot(
            k, crossed(spec[2 * k], spec[2 * k + 1]), crossed(spec_low[2 * k], spec_low[2 * k + 1])
        )
        fspec[k, :ROWS] = both[:, : HALVES * LANES]
        fspec[k, ROWS:] = both[:, HALVES * LANES :]

    slots(8, filter_lone, filter_inner)

    loads[3].wait()
    edge_out[2] = jnp.concatenate([part for h in range(HALVES) for part in last_rows(qbuf, h)], axis=0).astype(BF16)
    edge_copies[2].start()
    for i in (7, 8, 9):
        loads[i].wait()

    def feature_q(owner, carry):
        for h in range(HALVES):
            lanes = lanes_of(owner, h)
            before = [edges[h, i : i + 1, block_lanes(owner)] for i in (4, 5)]
            fbuf[owner, :, h * LANES : (h + 1) * LANES] = featurize(
                qbuf[:, lanes].astype(F32), tap_rows(0, lanes), before[0], before[1]
            )
        return carry

    def convolve(h):
        half = pl.ds(h * LANES, LANES)
        first = pl.ds(0, LANES)

        def signal_outer(g):
            rows = pl.ds(pl.multiple_of(16 * g, 16), 16)
            pairs = side_by_side(moved[h, :, rows, :].astype(F32), BLOCKS).astype(BF16)
            spec[:, rows, first] = stacked(dot(t_outer[0], pairs), 2 * BLOCKS).astype(BF16)

        loop(8, 8, signal_outer)

        def signal_lone():
            signal = spec[0:2, :, first].reshape(2 * ROWS, LANES)
            real, imag = dot(t_inner[0, 0], signal), dot(t_inner[0, BLOCKS], signal)
            f_real, f_imag = fspec[0, :ROWS, half], fspec[0, ROWS:, half]
            top = lax.broadcasted_iota(jnp.int32, (ROWS, LANES), 0) == 0
            f_last = jnp.where(top, f_imag, f_real)
            f_imag = jnp.where(top, 0.0, f_imag)
            product = jnp.concatenate([real * f_real - imag * f_imag, real * f_imag + imag * f_last], axis=0)
            product = product.astype(BF16)
            spec_low[0, :, first] = dot(t_inner_back[0], product).astype(BF16)
            spec_low[1, :, first] = dot(t_inner_back[BLOCKS], product).astype(BF16)

        def signal_inner(k):
            signal = dot(t_inner[0, k], crossed(spec[2 * k, :, first], spec[2 * k + 1, :, first]))
            real, imag = signal[:, :LANES], signal[:, LANES:]
            f_real, f_imag = fspec[k, :ROWS, half], fspec[k, ROWS:, half]
            up = (real * f_real - imag * f_imag).astype(BF16)
            across = (real * f_imag + imag * f_real).astype(BF16)
            restored = dot(t_inner_back[k], crossed(across, up)).astype(BF16)
            spec_low[2 * k, :, first] = restored[:, LANES:]
            spec_low[2 * k + 1, :, first] = restored[:, :LANES]

        slots(16, signal_lone, signal_inner)
        gain = sbuf[:, h * LANES : (h + 1) * LANES]

        def signal_back(g):
            rows = pl.ds(pl.multiple_of(16 * g, 16), 16)
            pairs = side_by_side(spec_low[:, rows, first].astype(F32), 2 * BLOCKS).astype(BF16)
            restored = stacked(dot(t_outer_back[...], pairs), BLOCKS)
            conv[h, :, rows, :] = (restored + gain * moved[h, :, rows, :].astype(F32)).astype(BF16)

        loop(8, 8, signal_back)

    for h in range(HALVES):
        for j, offset in enumerate(offsets()):
            origin = at(offset, -1)
            for copy in first_half(j, origin, origin) if h == 0 else [to_channels(1, origin, origin)]:
                copy.wait_recv()
        convolve(h)
        for offset in offsets():
            to_positions(h, at(offset), me).start()
        back[h, me] = conv[h, me]

    edge_copies[2].wait_recv()
    arrived_q = edge_in[2].astype(F32) * inside
    for h in range(HALVES):
        for s in range(4):
            row = 8 * h + 2 * s
            edges[h, 4:6, 1024 * s : 1024 * s + 1024] = arrived_q[row : row + 2]
    lax.fori_loop(0, BLOCKS, feature_q, 0)

    for j, offset in enumerate(offsets()):
        for copy in first_half(j, at(offset), me) + [to_channels(1, at(offset), me)]:
            copy.wait_send()
    for copy in edge_copies:
        copy.wait_send()

    def mix(h, origin):
        features = fbuf[origin, :, h * LANES : (h + 1) * LANES]
        out[:, lanes_of(origin, h)] = (features * back[h, origin].astype(F32)).astype(BF16)

    for h in range(HALVES):
        mix(h, me)
        for offset in offsets():
            origin = at(offset, -1)
            to_positions(h, origin, origin).wait_recv()
            mix(h, origin)
        for offset in offsets():
            to_positions(h, at(offset), me).wait_send()


def on_device(query_rows, key_rows, value_rows, short_taps, long_filter, skip_gain):
    rows, width = query_rows.shape
    outer, inner, inner_back, outer_back = transform_tables()
    tables = [high_low(outer), high_low(inner), high(inner_back), high(outer_back)]
    any_spec = pl.BlockSpec(memory_space=pl.ANY)
    dma = pltpu.SemaphoreType.DMA
    blocks = (HALVES, BLOCKS, ROWS, LANES)
    return pl.pallas_call(
        kernel,
        out_shape=pltpu.VMEM((rows, width), BF16),
        in_specs=[any_spec] * 10,
        out_specs=pl.BlockSpec(memory_space=pltpu.VMEM),
        scratch_shapes=[
            pltpu.VMEM((rows, width), BF16), pltpu.VMEM((rows, width), BF16), pltpu.VMEM((rows, width), BF16),
            pltpu.VMEM((3, 3, width), F32), pltpu.VMEM((BLOCKS, ROWS, HALVES * LANES), F32), pltpu.VMEM((1, HALVES * LANES), F32),
            *[pltpu.VMEM(t.shape, BF16) for t in tables],
            pltpu.VMEM((3, 16, 1024), BF16), pltpu.VMEM((3, 16, 1024), BF16), pltpu.VMEM((HALVES, 8, width // HALVES), F32),
            *[pltpu.VMEM(blocks, BF16)] * 4,
            *[pltpu.VMEM((2 * BLOCKS, ROWS, HALVES * LANES), BF16)] * 2,
            pltpu.VMEM((BLOCKS, 2 * ROWS, HALVES * LANES), F32),
            dma((12,)), dma((3,)), dma((3,)), *[dma((HALVES, BLOCKS))] * 2, *[dma((BLOCKS,))] * 2, *[dma((HALVES, BLOCKS))] * 2,
        ],
        compiler_params=pltpu.CompilerParams(collective_id=0, has_side_effects=True, vmem_limit_bytes=56 << 20),
        name="mixer",
    )(
        query_rows, key_rows, value_rows, short_taps, long_filter.reshape(BLOCKS, ROWS, HALVES * LANES),
        skip_gain.reshape(1, HALVES * LANES), *[jnp.asarray(t) for t in tables],
    )


def solution(mesh):
    in_specs = (P(("dp", "ctx"), None), P(("dp", "ctx"), None), P(("dp", "ctx"), None), P(), P(None, "ctx"), P("ctx"))
    return jax.shard_map(on_device, mesh=mesh, in_specs=in_specs, out_specs=P(("dp", "ctx"), None), check_vma=False)
```

```python
import functools

import jax
import jax.numpy as jnp
import ml_dtypes
import numpy as np
from jax import lax
from jax.experimental import pallas as pl
from jax.experimental.pallas import tpu as pltpu
from jax.sharding import PartitionSpec as P

F32, BF16 = jnp.float32, jnp.bfloat16
MESH = pl.DeviceIdType.MESH

BLOCKS, ROWS, LANES = 32, 128, 128
FULL = 2 * BLOCKS * ROWS
HALVES = 2


def transform_tables():
    p, k1 = np.arange(BLOCKS), np.arange(BLOCKS)
    angle = 2 * np.pi * (k1[:, None] * p % 64) / 64
    outer = np.zeros((BLOCKS, 2, BLOCKS))
    outer[:, 0], outer[:, 1] = np.cos(angle), -np.sin(angle)
    outer[0, 1] = np.cos(np.pi * p)
    outer_back = np.zeros((BLOCKS, BLOCKS, 2))
    outer_back[:, :, 0], outer_back[:, :, 1] = 2 * np.cos(angle.T), -2 * np.sin(angle.T)
    outer_back[:, 0, 0], outer_back[:, 0, 1] = 1, np.cos(np.pi * p)
    outer_back /= FULL
    r, k2 = np.arange(ROWS), np.arange(ROWS)
    inner = np.zeros((BLOCKS + 1, ROWS, 2 * ROWS))
    inner_back = np.zeros((BLOCKS + 1, ROWS, 2 * ROWS))
    for k in range(1, BLOCKS):
        turn = 2 * np.pi * ((k + 64 * k2)[:, None] * r % FULL) / FULL
        inner[k] = np.block([np.cos(turn), np.sin(turn)])
        inner_back[k] = np.block([np.cos(turn.T), np.sin(turn.T)])
    half = np.arange(64)[:, None]
    even = 2 * np.pi * (64 * half * r % FULL) / FULL
    odd = 2 * np.pi * ((32 + 64 * half) * r % FULL) / FULL
    lone = np.zeros((2 * ROWS, 2 * ROWS))
    lone[0:64, :ROWS], lone[64:128, ROWS:] = np.cos(even), np.cos(odd)
    lone[128:192, :ROWS], lone[192:256, ROWS:] = -np.sin(even), -np.sin(odd)
    lone[128, :ROWS] = np.cos(np.pi * r)
    weight = np.full(2 * ROWS, 2.0)
    weight[0] = weight[128] = 1
    inner[0], inner[BLOCKS] = lone[:ROWS], lone[ROWS:]
    inner_back[0], inner_back[BLOCKS] = (lone.T * weight)[:ROWS], (lone.T * weight)[ROWS:]
    eye = np.eye(8)
    outer = np.kron(outer.reshape(2 * BLOCKS, BLOCKS), eye)
    outer_back = np.kron(outer_back.reshape(BLOCKS, 2 * BLOCKS), eye)
    return outer, inner, inner_back, outer_back


def high_low(table):
    table = table.astype(np.float32)
    high = table.astype(ml_dtypes.bfloat16)
    return np.stack([high, (table - high.astype(np.float32)).astype(ml_dtypes.bfloat16)])


def high(table):
    return table.astype(np.float32).astype(ml_dtypes.bfloat16)


def dot(a, b):
    return jnp.dot(a, b, preferred_element_type=F32)


def split(a):
    top = a.astype(BF16)
    return top, (a - top.astype(F32)).astype(BF16)


def side_by_side(x, n):
    return jnp.concatenate([x[:, :8].reshape(8 * n, LANES), x[:, 8:].reshape(8 * n, LANES)], axis=1)


def stacked(z, n):
    return jnp.concatenate([z[:, :LANES].reshape(n, 8, LANES), z[:, LANES:].reshape(n, 8, LANES)], axis=1)


def crossed(real, imag):
    return jnp.concatenate(
        [jnp.concatenate([real, imag], axis=1), jnp.concatenate([imag, -real], axis=1)], axis=0
    )


def slots(step, lone, body):
    lone()
    for k in range(1, step):
        body(k)

    def several(j, carry):
        for i in range(step):
            body(j * step + i)
        return carry

    lax.fori_loop(1, BLOCKS // step, several, 0)


def loop(count, step, body):
    def several(j, carry):
        for i in range(step):
            body(j * step + i)
        return carry

    lax.fori_loop(0, count // step, several, 0)


def featurize(block, taps, edge_two, edge_one):
    row = lax.broadcasted_iota(jnp.int32, (8, LANES), 0)
    one, two = pltpu.roll(block, 1, 0), pltpu.roll(block, 2, 0)
    top_one = jnp.where(row == 0, edge_one, one[:8])
    top_two = jnp.where(row == 0, edge_two, jnp.where(row == 1, edge_one, two[:8]))
    one = jnp.concatenate([top_one, one[8:]], axis=0)
    two = jnp.concatenate([top_two, two[8:]], axis=0)
    return taps[0] * block + taps[1] * one + taps[2] * two


def offsets():
    def hops(o):
        return min(o[0], 4 - o[0]), min(o[1], 4 - o[1]), o[2]

    span = [(dx, dy, dz) for dy in range(4) for dz in range(2) for dx in range(4)]
    left = sorted(span, key=lambda o: -sum(hops(o)))[:-1]
    order = []
    while left:
        order.append(left.pop(0))
        along = hops(order[-1])
        rest = [o for o in left if hops(o) == (2 - along[0], 2 - along[1], 1 - along[2])]
        if rest:
            left.remove(rest[0])
            order.append(rest[0])
    return sorted(order, key=lambda o: o[1] % 2)


EARLY = 15


def kernel(
    query, key, value, short_taps, filt, skip, outer, inner, inner_back, outer_back, out,
    qbuf, kbuf, vbuf, taps, fbuf, sbuf, t_outer, t_inner, t_inner_back, t_outer_back,
    edge_out, edge_in, edges, gated, moved, conv, back, spec, spec_low, fspec,
    load_sem, edge_send, edge_recv, send_one, recv_one, send_top, recv_top, send_two, recv_two,
):
    me = lax.axis_index("ctx")
    x, z, y = me % 4, (me // 4) % 2, me // 8
    sign = 1 - 2 * (lax.axis_index("dp") % 2)

    def at(offset, way=1):
        dx, dy, dz = offset
        return ((y + 4 + way * sign * dy) % 4 * 2 + (z + dz) % 2) * 4 + (x + 4 + way * sign * dx) % 4

    ends = [
        pltpu.make_async_copy(src.at[pl.ds(ROWS - 16, 16)], dst.at[pl.ds(ROWS - 16, 16)], load_sem.at[10 + i])
        for i, (src, dst) in enumerate([(key, kbuf), (value, vbuf)])
    ]
    def quarter(src, dst, dy, slot):
        width = src.shape[1] // 4
        part = (pl.ds(0, ROWS - 16), pl.ds(pl.multiple_of((y + dy) % 4 * width, width), width))
        return pltpu.make_async_copy(src.at[part], dst.at[part], load_sem.at[slot])

    quarters = [
        quarter(src, dst, dy, 12 + 2 * i + n)
        for i, dy in enumerate((2, 0, 1, 3))
        for n, (src, dst) in enumerate([(key, kbuf), (value, vbuf)])
    ]
    loads = [
        pltpu.make_async_copy(src, dst, load_sem.at[i + 2])
        for i, (src, dst) in enumerate(
            [
                (short_taps, taps), (query, qbuf), (filt, fbuf), (outer, t_outer),
                (inner, t_inner), (skip, sbuf), (inner_back, t_inner_back), (outer_back, t_outer_back),
            ]
        )
    ]
    for load in ends:
        load.start()
    for load in [loads[0], *quarters]:
        load.start()

    barrier = pltpu.get_barrier_semaphore()

    def greet(j, carry):
        pl.semaphore_signal(barrier, inc=1, device_id={"ctx": (me + j) % BLOCKS}, device_id_type=MESH)
        return carry

    lax.fori_loop(1, BLOCKS, greet, 0)
    for load in ends:
        load.wait()

    def last_rows(buf, h):
        rows = buf[ROWS - 16 :, :].astype(F32)[14:16]
        picked = [rows[:, (HALVES * b + h) * LANES : (HALVES * b + h + 1) * LANES] for b in range(BLOCKS)]
        return [jnp.concatenate(picked[8 * s : 8 * s + 8], axis=1) for s in range(4)]

    following = {"ctx": (me + 1) % BLOCKS}
    edge_copies = [
        pltpu.make_async_remote_copy(
            src_ref=edge_out.at[i], dst_ref=edge_in.at[i], send_sem=edge_send.at[i], recv_sem=edge_recv.at[i],
            device_id=following, device_id_type=MESH,
        )
        for i in range(3)
    ]
    inside = jnp.where(me == 0, 0.0, 1.0)
    for h in range(HALVES):
        parts = [part for both in zip(last_rows(kbuf, h), last_rows(vbuf, h)) for part in both]
        edge_out[h] = jnp.concatenate(parts, axis=0).astype(BF16)

    def lanes_of(owner, h):
        return pl.ds(pl.multiple_of((HALVES * owner + h) * LANES, LANES), LANES)

    def block_lanes(owner):
        return pl.ds(pl.multiple_of(owner * LANES, LANES), LANES)

    def tap_rows(which, lanes):
        return [taps[which, i : i + 1, lanes] for i in range(3)]

    def gate(rows, owner, h):
        lanes = lanes_of(owner, h)
        if rows == 16:
            before = [edges[h, i : i + 1, block_lanes(owner)] for i in range(4)]
        else:
            before = [jnp.zeros((1, LANES), F32)] * 4
        fk = featurize(kbuf[:rows, lanes].astype(F32), tap_rows(1, lanes), before[0], before[1])
        fv = featurize(vbuf[:rows, lanes].astype(F32), tap_rows(2, lanes), before[2], before[3])
        return (fk * fv).astype(BF16)

    def copy_to(src, dst, send, recv, to, h, origin):
        return pltpu.make_async_remote_copy(
            src_ref=src.at[h, to], dst_ref=dst.at[h, origin], send_sem=send.at[h, to], recv_sem=recv.at[h, origin],
            device_id={"ctx": to}, device_id_type=MESH,
        )

    def to_channels(h, to, origin):
        return copy_to(gated, moved, send_one, recv_one, to, h, origin)

    def part_to_channels(rows, send, recv, to, origin):
        return pltpu.make_async_remote_copy(
            src_ref=gated.at[0, to, rows], dst_ref=moved.at[0, origin, rows], send_sem=send, recv_sem=recv,
            device_id={"ctx": to}, device_id_type=MESH,
        )

    def rest_to_channels(to, origin):
        return part_to_channels(pl.ds(16, ROWS - 16), send_one.at[0, to], recv_one.at[0, origin], to, origin)

    def top_to_channels(to, origin):
        return part_to_channels(pl.ds(0, 16), send_top.at[to], recv_top.at[origin], to, origin)

    def first_half(j, to, origin):
        if j < EARLY:
            return [rest_to_channels(to, origin), top_to_channels(to, origin)]
        return [to_channels(0, to, origin)]

    def to_positions(h, to, origin):
        return copy_to(conv, back, send_two, recv_two, to, h, origin)

    def gate_rest(h, owner):
        gated[h, owner, 16:] = gate(ROWS, owner, h)[16:]

    def gate_top(h):
        arrived = edge_in[h].astype(F32) * inside
        for s in range(4):
            edges[h, 0:4, 1024 * s : 1024 * s + 1024] = arrived[4 * s : 4 * s + 4]

        def one(owner, carry):
            gated[h, owner, :16] = gate(16, owner, h)
            return carry

        lax.fori_loop(0, BLOCKS, one, 0)

    for load in [loads[0], *quarters[:4]]:
        load.wait()
    pl.semaphore_wait(barrier, BLOCKS - 1)
    for h in range(HALVES):
        edge_copies[h].start()
    for offset in offsets()[:EARLY]:
        gate_rest(0, at(offset))
        rest_to_channels(at(offset), me).start()
    for i in (2, 3, 4):
        loads[i].start()
    for load in quarters[4:]:
        load.wait()
    for offset in offsets()[EARLY:]:
        gate_rest(0, at(offset))
    gate_rest(0, me)
    edge_copies[0].wait_recv()
    gate_top(0)
    for j, offset in enumerate(offsets()):
        first_half(j, at(offset), me)[-1].start()
    moved[0, me] = gated[0, me]

    def gate_second(owner, carry):
        gate_rest(1, owner)
        return carry

    lax.fori_loop(0, BLOCKS, gate_second, 0)
    edge_copies[1].wait_recv()
    gate_top(1)

    for i in (2, 3, 4):
        loads[i].wait()

    def filter_outer(g):
        turned = []
        for i in range(2):
            rows = pl.ds(pl.multiple_of(16 * g + 8 * i, 8), 8)
            top, low = split(fbuf[:, rows, :].reshape(8 * BLOCKS, HALVES * LANES))
            part = dot(t_outer[0], top) + dot(t_outer[1], top) + dot(t_outer[0], low)
            turned.append(part.reshape(2 * BLOCKS, 8, HALVES * LANES))
        top, low = split(jnp.concatenate(turned, axis=1))
        rows = pl.ds(pl.multiple_of(16 * g, 16), 16)
        spec[:, rows, :] = top
        spec_low[:, rows, :] = low

    loop(8, 2, filter_outer)
    for i in (5, 6, 7, 1):
        loads[i].start()
    for offset in offsets():
        to_channels(1, at(offset), me).start()
    moved[1, me] = gated[1, me]

    def filter_dot(k, top, low):
        return dot(t_inner[0, k], top) + dot(t_inner[1, k], top) + dot(t_inner[0, k], low)

    def filter_lone():
        top = spec[0:2].reshape(2 * ROWS, HALVES * LANES)
        low = spec_low[0:2].reshape(2 * ROWS, HALVES * LANES)
        fspec[0, :ROWS] = filter_dot(0, top, low)
        fspec[0, ROWS:] = filter_dot(BLOCKS, top, low)

    def filter_inner(k):
        both = filter_dot(
            k, crossed(spec[2 * k], spec[2 * k + 1]), crossed(spec_low[2 * k], spec_low[2 * k + 1])
        )
        fspec[k, :ROWS] = both[:, : HALVES * LANES]
        fspec[k, ROWS:] = both[:, HALVES * LANES :]

    slots(8, filter_lone, filter_inner)

    loads[1].wait()
    edge_out[2] = jnp.concatenate([part for h in range(HALVES) for part in last_rows(qbuf, h)], axis=0).astype(BF16)
    edge_copies[2].start()
    for i in (5, 6, 7):
        loads[i].wait()

    def feature_q(owner, carry):
        for h in range(HALVES):
            lanes = lanes_of(owner, h)
            before = [edges[h, i : i + 1, block_lanes(owner)] for i in (4, 5)]
            fbuf[owner, :, h * LANES : (h + 1) * LANES] = featurize(
                qbuf[:, lanes].astype(F32), tap_rows(0, lanes), before[0], before[1]
            )
        return carry

    def convolve(h):
        half = pl.ds(h * LANES, LANES)
        first = pl.ds(0, LANES)

        def signal_outer(g):
            rows = pl.ds(pl.multiple_of(16 * g, 16), 16)
            pairs = side_by_side(moved[h, :, rows, :].astype(F32), BLOCKS).astype(BF16)
            spec[:, rows, first] = stacked(dot(t_outer[0], pairs), 2 * BLOCKS).astype(BF16)

        loop(8, 8, signal_outer)

        def signal_lone():
            signal = spec[0:2, :, first].reshape(2 * ROWS, LANES)
            real, imag = dot(t_inner[0, 0], signal), dot(t_inner[0, BLOCKS], signal)
            f_real, f_imag = fspec[0, :ROWS, half], fspec[0, ROWS:, half]
            top = lax.broadcasted_iota(jnp.int32, (ROWS, LANES), 0) == 0
            f_last = jnp.where(top, f_imag, f_real)
            f_imag = jnp.where(top, 0.0, f_imag)
            product = jnp.concatenate([real * f_real - imag * f_imag, real * f_imag + imag * f_last], axis=0)
            product = product.astype(BF16)
            spec_low[0, :, first] = dot(t_inner_back[0], product).astype(BF16)
            spec_low[1, :, first] = dot(t_inner_back[BLOCKS], product).astype(BF16)

        def signal_inner(k):
            signal = dot(t_inner[0, k], crossed(spec[2 * k, :, first], spec[2 * k + 1, :, first]))
            real, imag = signal[:, :LANES], signal[:, LANES:]
            f_real, f_imag = fspec[k, :ROWS, half], fspec[k, ROWS:, half]
            up = (real * f_real - imag * f_imag).astype(BF16)
            across = (real * f_imag + imag * f_real).astype(BF16)
            restored = dot(t_inner_back[k], crossed(across, up)).astype(BF16)
            spec_low[2 * k, :, first] = restored[:, LANES:]
            spec_low[2 * k + 1, :, first] = restored[:, :LANES]

        slots(16, signal_lone, signal_inner)
        gain = sbuf[:, h * LANES : (h + 1) * LANES]

        def signal_back(g):
            rows = pl.ds(pl.multiple_of(16 * g, 16), 16)
            pairs = side_by_side(spec_low[:, rows, first].astype(F32), 2 * BLOCKS).astype(BF16)
            restored = stacked(dot(t_outer_back[...], pairs), BLOCKS)
            conv[h, :, rows, :] = (restored + gain * moved[h, :, rows, :].astype(F32)).astype(BF16)

        loop(8, 8, signal_back)

    for h in range(HALVES):
        for j, offset in enumerate(offsets()):
            origin = at(offset, -1)
            for copy in first_half(j, origin, origin) if h == 0 else [to_channels(1, origin, origin)]:
                copy.wait_recv()
        convolve(h)
        for offset in offsets():
            to_positions(h, at(offset), me).start()
        back[h, me] = conv[h, me]

    edge_copies[2].wait_recv()
    arrived_q = edge_in[2].astype(F32) * inside
    for h in range(HALVES):
        for s in range(4):
            row = 8 * h + 2 * s
            edges[h, 4:6, 1024 * s : 1024 * s + 1024] = arrived_q[row : row + 2]
    lax.fori_loop(0, BLOCKS, feature_q, 0)

    for j, offset in enumerate(offsets()):
        for copy in first_half(j, at(offset), me) + [to_channels(1, at(offset), me)]:
            copy.wait_send()
    for copy in edge_copies:
        copy.wait_send()

    def mix(h, origin):
        features = fbuf[origin, :, h * LANES : (h + 1) * LANES]
        out[:, lanes_of(origin, h)] = (features * back[h, origin].astype(F32)).astype(BF16)

    for h in range(HALVES):
        mix(h, me)
        for offset in offsets():
            origin = at(offset, -1)
            to_positions(h, origin, origin).wait_recv()
            mix(h, origin)
        for offset in offsets():
            to_positions(h, at(offset), me).wait_send()


def on_device(query_rows, key_rows, value_rows, short_taps, long_filter, skip_gain):
    rows, width = query_rows.shape
    outer, inner, inner_back, outer_back = transform_tables()
    tables = [high_low(outer), high_low(inner), high(inner_back), high(outer_back)]
    any_spec = pl.BlockSpec(memory_space=pl.ANY)
    dma = pltpu.SemaphoreType.DMA
    blocks = (HALVES, BLOCKS, ROWS, LANES)
    return pl.pallas_call(
        kernel,
        out_shape=pltpu.VMEM((rows, width), BF16),
        in_specs=[any_spec] * 10,
        out_specs=pl.BlockSpec(memory_space=pltpu.VMEM),
        scratch_shapes=[
            pltpu.VMEM((rows, width), BF16), pltpu.VMEM((rows, width), BF16), pltpu.VMEM((rows, width), BF16),
            pltpu.VMEM((3, 3, width), F32), pltpu.VMEM((BLOCKS, ROWS, HALVES * LANES), F32), pltpu.VMEM((1, HALVES * LANES), F32),
            *[pltpu.VMEM(t.shape, BF16) for t in tables],
            pltpu.VMEM((3, 16, 1024), BF16), pltpu.VMEM((3, 16, 1024), BF16), pltpu.VMEM((HALVES, 8, width // HALVES), F32),
            *[pltpu.VMEM(blocks, BF16)] * 4,
            *[pltpu.VMEM((2 * BLOCKS, ROWS, HALVES * LANES), BF16)] * 2,
            pltpu.VMEM((BLOCKS, 2 * ROWS, HALVES * LANES), F32),
            dma((20,)), dma((3,)), dma((3,)), *[dma((HALVES, BLOCKS))] * 2, *[dma((BLOCKS,))] * 2, *[dma((HALVES, BLOCKS))] * 2,
        ],
        compiler_params=pltpu.CompilerParams(collective_id=0, has_side_effects=True, vmem_limit_bytes=56 << 20),
        name="mixer",
    )(
        query_rows, key_rows, value_rows, short_taps, long_filter.reshape(BLOCKS, ROWS, HALVES * LANES),
        skip_gain.reshape(1, HALVES * LANES), *[jnp.asarray(t) for t in tables],
    )


def solution(mesh):
    in_specs = (P(("dp", "ctx"), None), P(("dp", "ctx"), None), P(("dp", "ctx"), None), P(), P(None, "ctx"), P("ctx"))
    return jax.shard_map(on_device, mesh=mesh, in_specs=in_specs, out_specs=P(("dp", "ctx"), None), check_vma=False)
```
